32 devices in a mesh: ctx: 8 (over y, x, core), grp: 4 (over z).
Axes of the slice: x: 2, y: 2, z: 4, core: 2. Of those that a mesh axis runs over, the one named last changes fastest.
Arguments:
- signal: bfloat16 [4096, 4096], P('ctx', 'grp'), may hold values from -6 to 6
- gate: bfloat16 [4096, 4096], P('ctx', 'grp'), may hold values from -6 to 6
- filter_taps: bfloat16 [4096, 512], P('ctx', 'grp'), may hold values from -0.09375 to 0.09375
- skip_gain: float32 [4096], P('grp'), may hold values from -4 to 4
- out_cotangent: bfloat16 [4096, 4096], P('ctx', 'grp'), may hold values from -6 to 6
Outputs:
- output: bfloat16 [4096, 4096], P('ctx', 'grp')
- grad_gate: bfloat16 [4096, 4096], P('ctx', 'grp')
- grad_signal: bfloat16 [4096, 4096], P('ctx', 'grp')
- grad_filter: float32 [4096, 512], P('ctx', 'grp')
The draws below stay inside these ranges and needn't reach their ends.
All inputs are finite; a program needn't handle non-finite values.
Results may differ from the reference program's by a relative error of at most 0.011.
Values may be sent and summed in bfloat16 or wider, within the bound.
A program may use at most 192 MiB of HBM per device.

```python
import math
import jax
import jax.numpy as jnp
from jax import lax

C = 4096
FG = 512
TOK_DEV = 512
SEQ = 4096
N_CTX = 8


def block_scale(own_key, shape, cuts, low, top_value):
    def one(position, parts):
        heights = jax.random.uniform(jax.random.fold_in(jax.random.fold_in(own_key, 6), position), (parts,), jnp.float32, low / len(cuts), top_value / len(cuts))
        return jnp.repeat(jnp.exp(heights), shape[position] // parts).reshape((-1,) + (1,) * (len(shape) - position - 1))

    gain = one(*cuts[0])
    for cut in cuts[1:]:
        gain = gain * one(*cut)
    return gain


def noise(own_key, shape, scale, limit, cuts=(), held_as=jnp.bfloat16):
    values = jax.random.normal(own_key, shape, jnp.float32) * scale
    if len(cuts) > 0:
        values = block_scale(own_key, shape, cuts, -0.22, 0.18) * values
    return jnp.clip(values, min=-limit, max=limit).astype(held_as)


def setup_inputs(seed: int = 0) -> dict:
    seeds = jax.random.split(jax.random.key(seed), 6)
    return {
        "signal": noise(seeds[0], (SEQ, C), 1.0, 6.0, ((0, 8), (1, 4))),
        "gate": noise(seeds[1], (SEQ, C), 1.0, 6.0, ((0, 8), (1, 4))),
        "filter_taps": noise(seeds[2], (SEQ, FG), SEQ ** -0.5, 0.09375, ((0, 8), (1, 4))),
        "skip_gain": noise(seeds[3], (C,), 1.0, 4.0, ((0, 4),), jnp.float32),
        "out_cotangent": noise(seeds[4], (SEQ, C), 1.0, 6.0, ((0, 8), (1, 4))),
    }


TWO_PI = 2.0 * math.pi

def phase_pair(first_index, second_index, length):
    products_mod = first_index[:, None] * second_index[None, :] % length
    angles = products_mod.astype(jnp.float32) * (TWO_PI / length)
    return (jnp.cos(angles), -jnp.sin(angles))

def build_tables(devices_count, block_length, table_type):
    first_length = 2 * devices_count
    cosine_first, sine_first = phase_pair(jnp.arange(first_length, dtype=jnp.int32), jnp.arange(devices_count, dtype=jnp.int32), first_length)
    stacked_rows = jnp.concatenate([cosine_first, sine_first], axis=0).astype(table_type)
    paired_rows = jnp.stack([cosine_first, sine_first], axis=0).astype(table_type)
    cosine_rows, sine_rows = phase_pair(jnp.arange(block_length, dtype=jnp.int32), jnp.arange(block_length, dtype=jnp.int32), block_length)
    return (stacked_rows, paired_rows, cosine_rows.astype(table_type), sine_rows.astype(table_type))

def matmul_exact(form, left_side, right_side):
    return jnp.einsum(form, left_side.astype(jnp.float32), right_side.astype(jnp.float32), precision=lax.Precision.HIGHEST, preferred_element_type=jnp.float32)

def rotate_forward(first_out, first_freq, within_block, padded):
    half_rows = first_out.shape[0] // 2
    real_part = first_out[:half_rows]
    imag_part = first_out[half_rows:]
    twiddle_real, twiddle_imag = phase_pair(first_freq, within_block, padded)
    twiddle_real = twiddle_real[:, :, None]
    twiddle_imag = twiddle_imag[:, :, None]
    return jnp.stack([real_part * twiddle_real - imag_part * twiddle_imag, real_part * twiddle_imag + imag_part * twiddle_real])

def transform(values, tables, devices_count, block_length):
    stacked_rows, paired_rows, cosine_rows, sine_rows = tables
    padded = 2 * devices_count * block_length
    shaped = values.reshape(devices_count, block_length, values.shape[1])
    first_out = matmul_exact('ka,abc->kbc', stacked_rows, shaped)
    rotated = rotate_forward(first_out, jnp.arange(2 * devices_count, dtype=jnp.int32), jnp.arange(block_length, dtype=jnp.int32), padded).astype(jnp.bfloat16)
    with_cosine = matmul_exact('jb,pkbc->pkjc', cosine_rows, rotated)
    with_sine = matmul_exact('jb,pkbc->pkjc', sine_rows, rotated)
    return jnp.stack([with_cosine[0] - with_sine[1], with_cosine[1] + with_sine[0]])

def inverse(spectra, tables, devices_count, block_length, precise):
    stacked_rows, paired_rows, cosine_rows, sine_rows = tables
    padded = 2 * devices_count * block_length
    operand = spectra if precise else spectra.astype(jnp.bfloat16)
    with_cosine = matmul_exact('jb,pkjc->pkbc', cosine_rows, operand)
    with_sine = matmul_exact('jb,pkjc->pkbc', sine_rows, operand)
    real_turned = with_cosine[0] + with_sine[1]
    imag_turned = with_cosine[1] - with_sine[0]
    twiddle_real, twiddle_imag = phase_pair(jnp.arange(2 * devices_count, dtype=jnp.int32), jnp.arange(block_length, dtype=jnp.int32), padded)
    twiddle_real = twiddle_real[:, :, None]
    twiddle_imag = twiddle_imag[:, :, None]
    rotated = jnp.stack([real_turned * twiddle_real + imag_turned * twiddle_imag, imag_turned * twiddle_real - real_turned * twiddle_imag])
    if not precise:
        rotated = rotated.astype(jnp.bfloat16)
    rows_out = matmul_exact('pka,pkbc->abc', paired_rows, rotated) * (1.0 / padded)
    return rows_out.reshape(devices_count * block_length, rows_out.shape[2])

def spectral_products(spectra, filter_low, width):
    filter_wide = filter_low.astype(jnp.float32)
    filter_real = filter_wide[0]
    filter_imag = filter_wide[1]
    input_real = spectra[0, ..., :width]
    input_imag = spectra[1, ..., :width]
    grad_real = spectra[0, ..., width:]
    grad_imag = spectra[1, ..., width:]
    channel_terms = jnp.stack([jnp.concatenate([input_real * filter_real - input_imag * filter_imag, grad_real * filter_real + grad_imag * filter_imag], axis=-1), jnp.concatenate([input_real * filter_imag + input_imag * filter_real, grad_imag * filter_real - grad_real * filter_imag], axis=-1)])
    filter_term = jnp.stack([input_real * grad_real + input_imag * grad_imag, input_real * grad_imag - input_imag * grad_real])
    return (channel_terms, filter_term)

def reference(signal, gate, filter_taps, skip_gain, out_cotangent):
    devices_count = N_CTX
    block_length = TOK_DEV
    repeats = C // FG
    coarse_tables = build_tables(devices_count, block_length, jnp.bfloat16)
    exact_tables = build_tables(devices_count, block_length, jnp.float32)
    gated = (out_cotangent.astype(jnp.float32) * gate.astype(jnp.float32)).astype(jnp.bfloat16)
    filter_low = lax.optimization_barrier(transform(filter_taps, coarse_tables, devices_count, block_length).astype(jnp.bfloat16))

    def block_step(totals, pieces):
        input_block, gated_block, gate_block, cotangent_block, gain_block = pieces
        spectra = transform(jnp.concatenate([input_block, gated_block], axis=1), coarse_tables, devices_count, block_length)
        channel_terms, filter_term = spectral_products(spectra, filter_low, FG)
        signal_back = inverse(channel_terms, coarse_tables, devices_count, block_length, False)
        conv_part = signal_back[:, :FG] + gain_block[None, :] * input_block.astype(jnp.float32)
        output = (gate_block.astype(jnp.float32) * conv_part).astype(jnp.bfloat16)
        grad_gate = (cotangent_block.astype(jnp.float32) * conv_part).astype(jnp.bfloat16)
        grad_signal = (signal_back[:, FG:] + gain_block[None, :] * gated_block.astype(jnp.float32)).astype(jnp.bfloat16)
        return (totals + filter_term, (output, grad_gate, grad_signal))

    def split_blocks(array):
        return array.reshape(SEQ, repeats, FG).transpose(1, 0, 2)
    pieces = (split_blocks(signal), split_blocks(gated), split_blocks(gate), split_blocks(out_cotangent), skip_gain.reshape(repeats, FG))
    initial = jnp.zeros((2, 2 * devices_count, block_length, FG), jnp.float32)
    totals, outputs = lax.scan(block_step, initial, pieces)

    def join_blocks(stacked):
        return stacked.transpose(1, 0, 2).reshape(SEQ, C)
    grad_filter = inverse(totals, exact_tables, devices_count, block_length, True) * (1.0 / math.sqrt(SEQ * repeats))
    return (join_blocks(outputs[0]), join_blocks(outputs[1]), join_blocks(outputs[2]), grad_filter)
```

```python
import math

import jax
import jax.numpy as jnp
import ml_dtypes
import numpy as np
from jax import lax
from jax.experimental import pallas as pl
from jax.experimental.pallas import tpu as pltpu
from jax.sharding import PartitionSpec as P

TWO_PI = 2.0 * math.pi


def phase_pair(first_index, second_index, length):
    products_mod = first_index[:, None] * second_index[None, :] % length
    angles = products_mod.astype(jnp.float32) * (TWO_PI / length)
    return (jnp.cos(angles), -jnp.sin(angles))


def build_tables(devices_count, block_length, table_type):
    first_length = 2 * devices_count
    cosine_first, sine_first = phase_pair(
        jnp.arange(first_length, dtype=jnp.int32),
        jnp.arange(devices_count, dtype=jnp.int32),
        first_length,
    )
    stacked_rows = jnp.concatenate([cosine_first, sine_first], axis=0).astype(table_type)
    paired_rows = jnp.stack([cosine_first, sine_first], axis=0).astype(table_type)
    cosine_rows, sine_rows = phase_pair(
        jnp.arange(block_length, dtype=jnp.int32),
        jnp.arange(block_length, dtype=jnp.int32),
        block_length,
    )
    return (stacked_rows, paired_rows, cosine_rows.astype(table_type), sine_rows.astype(table_type))


def rotate_forward(first_out, first_freq, within_block, padded):
    half_rows = first_out.shape[0] // 2
    real_part = first_out[:half_rows]
    imag_part = first_out[half_rows:]
    twiddle_real, twiddle_imag = phase_pair(first_freq, within_block, padded)
    twiddle_real = twiddle_real[:, :, None]
    twiddle_imag = twiddle_imag[:, :, None]
    return jnp.stack(
        [
            real_part * twiddle_real - imag_part * twiddle_imag,
            real_part * twiddle_imag + imag_part * twiddle_real,
        ]
    )


def second_forward(rotated, cosine_rows, sine_rows):
    with_cosine = jnp.einsum(
        "jb,pkbc->pkjc", cosine_rows, rotated, preferred_element_type=jnp.float32
    )
    with_sine = jnp.einsum("jb,pkbc->pkjc", sine_rows, rotated, preferred_element_type=jnp.float32)
    return jnp.stack([with_cosine[0] - with_sine[1], with_cosine[1] + with_sine[0]])


def inverse_front(spectra, cosine_rows, sine_rows, first_freq, padded, precise):
    precision = lax.Precision.HIGHEST if precise else None
    operand = spectra if precise else spectra.astype(jnp.bfloat16)
    with_cosine = jnp.einsum(
        "jb,pkjc->pkbc",
        cosine_rows,
        operand,
        preferred_element_type=jnp.float32,
        precision=precision,
    )
    with_sine = jnp.einsum(
        "jb,pkjc->pkbc", sine_rows, operand, preferred_element_type=jnp.float32, precision=precision
    )
    real_turned = with_cosine[0] + with_sine[1]
    imag_turned = with_cosine[1] - with_sine[0]
    twiddle_real, twiddle_imag = phase_pair(
        first_freq, jnp.arange(spectra.shape[2], dtype=jnp.int32), padded
    )
    twiddle_real = twiddle_real[:, :, None]
    twiddle_imag = twiddle_imag[:, :, None]
    rotated = jnp.stack(
        [
            real_turned * twiddle_real + imag_turned * twiddle_imag,
            imag_turned * twiddle_real - real_turned * twiddle_imag,
        ]
    )
    if precise:
        return rotated
    return rotated.astype(jnp.bfloat16)


def inverse_back(rotated, paired_rows, padded, precise):
    precision = lax.Precision.HIGHEST if precise else None
    rows_out = jnp.einsum(
        "pka,pkbc->abc",
        paired_rows,
        rotated,
        preferred_element_type=jnp.float32,
        precision=precision,
    )
    return rows_out * (1.0 / padded)


def spectral_products(spectra, filter_low, width):
    filter_wide = filter_low.astype(jnp.float32)
    filter_real = filter_wide[0]
    filter_imag = filter_wide[1]
    input_real = spectra[0, ..., :width]
    input_imag = spectra[1, ..., :width]
    grad_real = spectra[0, ..., width:]
    grad_imag = spectra[1, ..., width:]
    channel_terms = jnp.stack(
        [
            jnp.concatenate(
                [
                    input_real * filter_real - input_imag * filter_imag,
                    grad_real * filter_real + grad_imag * filter_imag,
                ],
                axis=-1,
            ),
            jnp.concatenate(
                [
                    input_real * filter_imag + input_imag * filter_real,
                    grad_imag * filter_real - grad_real * filter_imag,
                ],
                axis=-1,
            ),
        ]
    )
    filter_term = jnp.stack(
        [
            input_real * grad_real + input_imag * grad_imag,
            input_real * grad_imag - input_imag * grad_real,
        ]
    )
    return (channel_terms, filter_term)


def split_forward(values, tables, position):
    stacked_rows, paired_rows, cosine_rows, sine_rows = tables
    devices_count = lax.axis_size("ctx")
    block_length = values.shape[0]
    lane_count = block_length // devices_count
    padded = 2 * devices_count * block_length
    first_length = 2 * devices_count
    first_out = jnp.einsum(
        "ka,abc->kbc",
        stacked_rows,
        lax.all_to_all(values[None], "ctx", split_axis=1, concat_axis=0, tiled=True),
        preferred_element_type=jnp.float32,
    )
    within_block = position * lane_count + jnp.arange(lane_count, dtype=jnp.int32)
    rotated = rotate_forward(
        first_out, jnp.arange(first_length, dtype=jnp.int32), within_block, padded
    ).astype(jnp.bfloat16)
    return second_forward(
        lax.all_to_all(rotated, "ctx", split_axis=1, concat_axis=2, tiled=True),
        cosine_rows,
        sine_rows,
    )


def split_inverse(spectra, tables, position, precise):
    stacked_rows, paired_rows, cosine_rows, sine_rows = tables
    devices_count = lax.axis_size("ctx")
    freq_count = spectra.shape[1]
    padded = 2 * devices_count * spectra.shape[2]
    first_freq = position * freq_count + jnp.arange(freq_count, dtype=jnp.int32)
    rotated = inverse_front(spectra, cosine_rows, sine_rows, first_freq, padded, precise)
    if precise:
        last_rows_out = inverse_back(
            lax.all_to_all(
                rotated.astype(jnp.bfloat16), "ctx", split_axis=2, concat_axis=1, tiled=True
            ).astype(rotated.dtype),
            paired_rows,
            padded,
            True,
        )
        result = lax.all_to_all(
            last_rows_out.astype(jnp.bfloat16), "ctx", split_axis=0, concat_axis=1, tiled=True
        ).astype(last_rows_out.dtype)
    else:
        rows_out = inverse_back(
            lax.all_to_all(rotated, "ctx", split_axis=2, concat_axis=1, tiled=True),
            paired_rows,
            padded,
            False,
        )
        result = lax.all_to_all(
            rows_out.astype(jnp.bfloat16), "ctx", split_axis=0, concat_axis=1, tiled=True
        ).astype(rows_out.dtype)
    return result[0]


def per_device_general(signal, gate, filter_taps, skip_gain, out_cotangent):
    devices_count = lax.axis_size("ctx")
    group_count = lax.axis_size("grp")
    block_length = signal.shape[0]
    local_channels = signal.shape[1]
    filters = filter_taps.shape[1] * group_count
    repeats = local_channels // filters
    position = lax.axis_index("ctx")
    coarse_tables = build_tables(devices_count, block_length, jnp.bfloat16)
    exact_tables = build_tables(devices_count, block_length, jnp.float32)
    gated = (out_cotangent.astype(jnp.float32) * gate.astype(jnp.float32)).astype(jnp.bfloat16)
    gain_wide = skip_gain[None, :]
    all_filters = lax.all_gather(filter_taps, "grp", axis=1, tiled=True)
    filter_low = lax.optimization_barrier(
        split_forward(all_filters, coarse_tables, position).astype(jnp.bfloat16)
    )
    filter_totals = jnp.zeros((2, 2, block_length, filters), jnp.float32)
    conv_blocks = []
    grad_blocks = []
    for block_index in range(repeats):
        lower = block_index * filters
        columns = jnp.concatenate(
            [signal[:, lower : lower + filters], gated[:, lower : lower + filters]], axis=1
        )
        spectra = split_forward(columns, coarse_tables, position)
        channel_terms, filter_term = spectral_products(spectra, filter_low, filters)
        filter_totals = filter_totals + filter_term
        signal_back = split_inverse(channel_terms, coarse_tables, position, False)
        conv_blocks.append(signal_back[:, :filters])
        grad_blocks.append(signal_back[:, filters:])
    conv_part = jnp.concatenate(conv_blocks, axis=1)
    grad_conv = jnp.concatenate(grad_blocks, axis=1)
    filter_back = split_inverse(filter_totals, exact_tables, position, True)
    grad_filter = lax.psum_scatter(
        filter_back.astype(jnp.bfloat16), "grp", scatter_dimension=1, tiled=True
    ).astype(jnp.float32)
    conv_part = conv_part + gain_wide * signal.astype(jnp.float32)
    output = (gate.astype(jnp.float32) * conv_part).astype(jnp.bfloat16)
    grad_gate = (out_cotangent.astype(jnp.float32) * conv_part).astype(jnp.bfloat16)
    grad_signal = (grad_conv + gain_wide * gated.astype(jnp.float32)).astype(jnp.bfloat16)
    scale = 1.0 / math.sqrt(devices_count * block_length * local_channels * group_count / filters)
    return (output, grad_gate, grad_signal, grad_filter * scale)


CTX = 8
FIRST = 16
ROWS = 512
LANES = 128
HALF = 64
STRIP = 16


def low(values):
    return np.asarray(values, np.float32).astype(ml_dtypes.bfloat16)


def first_coefficients():
    index = np.arange(FIRST)
    angles = (index[:, None] * index[None, :] % FIRST).astype(np.float32) * np.float32(TWO_PI / FIRST)
    return (
        low(np.round(np.cos(angles), 7)).astype(np.float64),
        low(np.round(np.sin(angles), 7)).astype(np.float64),
    )


def dense_tables():
    index = np.arange(ROWS)
    angles = (index[:, None] * index[None, :] % ROWS).astype(np.float32) * np.float32(TWO_PI / ROWS)
    wide = low(np.cos(angles)).astype(np.float64) - 1j * low(np.sin(angles)).astype(np.float64)
    freq = np.arange(FIRST)
    padded = FIRST * ROWS
    turn = np.exp(-2j * np.pi * (freq[:, None] * index[None, :] % padded) / padded)
    both = wide[None] * turn[:, None, :]
    forward = low(np.concatenate([both.real, both.imag], axis=2))
    back = both.transpose(0, 2, 1) / padded
    inverse = low(np.concatenate([back.real, -back.imag], axis=2))
    return forward, inverse


COS, SIN = first_coefficients()


def scaled_sum(terms):
    total = None
    for coefficient, value in terms:
        coefficient = float(coefficient)
        if abs(coefficient) < 1e-6:
            continue
        if total is None:
            total = value if coefficient == 1.0 else value * coefficient
        elif coefficient == 1.0:
            total = total + value
        elif coefficient == -1.0:
            total = total - value
        else:
            total = total + value * coefficient
    return total


def lower_half(shape):
    return lax.broadcasted_iota(jnp.int32, shape, len(shape) - 1) < HALF


def swap(values):
    return pltpu.roll(values, HALF, axis=1)


def times_i(values, sign):
    return swap(values) * sign


def forward_first(blocks, sign):
    plus = {a: blocks[a] + blocks[8 - a] for a in (1, 2, 3)}
    minus = {a: blocks[a] - blocks[8 - a] for a in (1, 2, 3)}
    results = [None] * FIRST
    for k in range(9):
        if k % 2 == 0:
            real = scaled_sum(
                [(1.0, blocks[0]), (COS[k, 4], blocks[4])] + [(COS[k, a], plus[a]) for a in (1, 2, 3)]
            )
            turned = scaled_sum([(-SIN[k, a], minus[a]) for a in (1, 2, 3)])
        else:
            real = scaled_sum([(1.0, blocks[0])] + [(COS[k, a], minus[a]) for a in (1, 2, 3)])
            turned = scaled_sum([(-SIN[k, 4], blocks[4])] + [(-SIN[k, a], plus[a]) for a in (1, 2, 3)])
        if turned is None:
            results[k] = real
            continue
        turned = times_i(turned, sign)
        results[k] = real + turned
        results[FIRST - k] = real - turned
    return results


def inverse_last(parts, sign):
    even = {k: parts[k] + parts[FIRST - k] for k in range(1, 8)}
    odd = {k: parts[k] - parts[FIRST - k] for k in range(1, 8)}
    results = [None] * CTX
    for a in range(5):
        flip = 1.0 if a % 2 == 0 else -1.0
        real_even = scaled_sum(
            [(1.0, parts[0]), (flip, parts[8])] + [(COS[k, a], even[k]) for k in (2, 4, 6)]
        )
        real_odd = scaled_sum([(COS[k, a], even[k]) for k in (1, 3, 5, 7)])
        turn_even = scaled_sum([(SIN[k, a], odd[k]) for k in (2, 4, 6)])
        turn_odd = scaled_sum([(SIN[k, a], odd[k]) for k in (1, 3, 5, 7)])
        real = real_even if real_odd is None else real_even + real_odd
        if a == 0:
            results[0] = real
            continue
        if a == 4:
            results[4] = real + times_i(turn_odd, sign)
            continue
        results[a] = real + times_i(turn_even + turn_odd, sign)
        results[8 - a] = (real_even - real_odd) + times_i(turn_odd - turn_even, sign)
    return results


def signs():
    return jnp.where(lower_half((1, LANES)), -1.0, 1.0).astype(jnp.float32)


def store_stacked(ref, k, rows, lanes, values, sign):
    top = pl.ds(rows, values.shape[0])
    bottom = pl.ds(ROWS + rows, values.shape[0])
    ref[k, top, lanes] = values.astype(jnp.bfloat16)
    ref[k, bottom, lanes] = times_i(values, sign).astype(jnp.bfloat16)


def stage_one(load, stacked_ref, lane_start):
    sign = signs()

    @pl.loop(0, ROWS // STRIP)
    def _(strip):
        rows = pl.multiple_of(strip * STRIP, STRIP)
        blocks = [load(a, pl.ds(rows, STRIP)) for a in range(CTX)]
        for k, values in enumerate(forward_first(blocks, sign)):
            store_stacked(
                stacked_ref, k, rows, slice(lane_start, lane_start + LANES), values, sign
            )


def last_stage(half_ref, lane_start, store):
    sign = signs()

    @pl.loop(0, ROWS // STRIP)
    def _(strip):
        rows = pl.multiple_of(strip * STRIP, STRIP)
        parts = [
            half_ref[k, pl.ds(rows, STRIP), lane_start : lane_start + LANES].astype(jnp.float32)
            for k in range(FIRST)
        ]
        for a, values in enumerate(inverse_last(parts, sign)):
            store(a, pl.ds(rows, STRIP), values)


def conv_kernel(signal_ref, taps_ref, forward_ref, inverse_ref, conv_ref, spec_ref, filt_ref,
                stacked, half):
    k = pl.program_id(0)

    @pl.when(k == 0)
    def _():
        stage_one(lambda a, rows: signal_ref[a, rows, :].astype(jnp.float32), stacked, 0)

        def load_taps(a, rows):
            values = taps_ref[a, rows, :].astype(jnp.float32)
            return jnp.concatenate([values, jnp.zeros_like(values)], axis=1)

        stage_one(load_taps, stacked, LANES)

    sign = signs()
    spectra = jnp.dot(forward_ref[0], stacked[k], preferred_element_type=jnp.float32)
    signal_spec = spectra[:, :LANES]
    filter_low = spectra[:, LANES:].astype(jnp.bfloat16)
    spec_ref[0] = signal_spec.astype(jnp.bfloat16)
    filt_ref[0] = filter_low
    filter_wide = filter_low.astype(jnp.float32)
    swapped = swap(filter_wide)
    first_half = lower_half((ROWS, LANES))
    filter_real = jnp.where(first_half, filter_wide, swapped)
    filter_imag = jnp.where(first_half, swapped, filter_wide)
    product = signal_spec * filter_real + times_i(signal_spec, sign) * filter_imag
    operand = jnp.concatenate([product, times_i(product, sign)], axis=0).astype(jnp.bfloat16)
    half[k] = jnp.dot(inverse_ref[0], operand, preferred_element_type=jnp.float32).astype(
        jnp.bfloat16
    )

    @pl.when(k == FIRST - 1)
    def _():
        def store(a, rows, values):
            conv_ref[a, rows, :] = values.astype(jnp.bfloat16)

        last_stage(half, 0, store)


def grad_kernel(gated_ref, spec_ref, filt_ref, forward_ref, inverse_ref, grad_ref, taps_ref,
                stacked, half):
    k = pl.program_id(0)

    @pl.when(k == 0)
    def _():
        stage_one(lambda a, rows: gated_ref[a, rows, :].astype(jnp.float32), stacked, 0)

    sign = signs()
    spectra = jnp.dot(forward_ref[0], stacked[k], preferred_element_type=jnp.float32)
    turned = times_i(spectra, sign)
    first_half = lower_half((ROWS, LANES))

    def split(values):
        swapped = swap(values)
        return jnp.where(first_half, values, swapped), jnp.where(first_half, swapped, values)

    filter_real, filter_imag = split(filt_ref[0].astype(jnp.float32))
    signal_real, signal_imag = split(spec_ref[0].astype(jnp.float32))
    back = spectra * filter_real - turned * filter_imag
    cross = spectra * signal_real - turned * signal_imag
    operand = jnp.concatenate(
        [
            jnp.concatenate([back, cross], axis=1),
            jnp.concatenate([times_i(back, sign), times_i(cross, sign)], axis=1),
        ],
        axis=0,
    ).astype(jnp.bfloat16)
    half[k] = jnp.dot(inverse_ref[0], operand, preferred_element_type=jnp.float32).astype(
        jnp.bfloat16
    )

    @pl.when(k == FIRST - 1)
    def _():
        def store(a, rows, values):
            grad_ref[a, rows, :] = values.astype(jnp.bfloat16)

        def store_taps(a, rows, values):
            taps_ref[a, rows, :] = values[:, :HALF].astype(jnp.bfloat16)

        last_stage(half, 0, store)
        last_stage(half, LANES, store_taps)


def whole_spec(shape):
    return pl.BlockSpec(shape, lambda k: (0,) * len(shape))


def each_spec(shape):
    return pl.BlockSpec((1,) + shape, lambda k: (k,) + (0,) * len(shape))


TABLE_SPEC = each_spec((ROWS, 2 * ROWS))
PARAMS = pltpu.CompilerParams(vmem_limit_bytes=56 * 1024 * 1024)
WORK = 2 * FIRST * ROWS * 2 * ROWS * 2 * LANES * 2
COST = pl.CostEstimate(flops=WORK, bytes_accessed=40 * 1024 * 1024, transcendentals=0)


def conv_call(signal_blocks, taps_blocks, forward, inverse):
    block = (CTX, ROWS, LANES)
    return pl.pallas_call(
        conv_kernel,
        grid=(FIRST,),
        in_specs=[whole_spec(block), whole_spec((CTX, ROWS, HALF)), TABLE_SPEC, TABLE_SPEC],
        out_specs=[whole_spec(block), each_spec((ROWS, LANES)), each_spec((ROWS, LANES))],
        out_shape=[
            jax.ShapeDtypeStruct(block, jnp.bfloat16),
            jax.ShapeDtypeStruct((FIRST, ROWS, LANES), jnp.bfloat16),
            jax.ShapeDtypeStruct((FIRST, ROWS, LANES), jnp.bfloat16),
        ],
        scratch_shapes=[
            pltpu.VMEM((FIRST, 2 * ROWS, 2 * LANES), jnp.bfloat16),
            pltpu.VMEM((FIRST, ROWS, LANES), jnp.bfloat16),
        ],
        compiler_params=PARAMS,
        cost_estimate=COST,
        name="conv_part",
    )(signal_blocks, taps_blocks, forward, inverse)


def grad_call(gated_blocks, spec, filt, forward, inverse):
    block = (CTX, ROWS, LANES)
    return pl.pallas_call(
        grad_kernel,
        grid=(FIRST,),
        in_specs=[
            whole_spec(block),
            each_spec((ROWS, LANES)),
            each_spec((ROWS, LANES)),
            TABLE_SPEC,
            TABLE_SPEC,
        ],
        out_specs=[whole_spec(block), whole_spec((CTX, ROWS, HALF))],
        out_shape=[
            jax.ShapeDtypeStruct(block, jnp.bfloat16),
            jax.ShapeDtypeStruct((CTX, ROWS, HALF), jnp.bfloat16),
        ],
        scratch_shapes=[
            pltpu.VMEM((FIRST, 2 * ROWS, LANES), jnp.bfloat16),
            pltpu.VMEM((FIRST, ROWS, 2 * LANES), jnp.bfloat16),
        ],
        compiler_params=PARAMS,
        cost_estimate=COST,
        name="grad_part",
    )(gated_blocks, spec, filt, forward, inverse)


def pack_pair(values, p):
    offset = CTX * HALF
    return jnp.concatenate(
        [values[:, HALF * p : HALF * p + HALF], values[:, offset + HALF * p : offset + HALF * p + HALF]],
        axis=1,
    )


def pack_kernel(signal_ref, packed_ref):
    values = signal_ref[...].astype(jnp.float32)
    for p in range(CTX):
        packed_ref[p] = pack_pair(values, p).astype(jnp.bfloat16)


def pack_gated_kernel(gate_ref, cotangent_ref, packed_ref):
    values = cotangent_ref[...].astype(jnp.float32) * gate_ref[...].astype(jnp.float32)
    for p in range(CTX):
        packed_ref[p] = pack_pair(values, p).astype(jnp.bfloat16)


PACK_ROWS = 128


def row_spec(width):
    return pl.BlockSpec((PACK_ROWS, width), lambda i: (i, 0))


def packed_spec():
    return pl.BlockSpec((CTX, PACK_ROWS, LANES), lambda i: (0, i, 0))


def pack_call(body, arrays):
    return pl.pallas_call(
        body,
        grid=(ROWS // PACK_ROWS,),
        in_specs=[row_spec(array.shape[1]) for array in arrays],
        out_specs=packed_spec(),
        out_shape=jax.ShapeDtypeStruct((CTX, ROWS, LANES), jnp.bfloat16),
        name="pack",
    )(*arrays)


def unpack(ref):
    blocks = [ref[p].astype(jnp.float32) for p in range(CTX)]
    return jnp.concatenate(
        [block[:, :HALF] for block in blocks] + [block[:, HALF:] for block in blocks], axis=1
    )


def outputs_kernel(conv_ref, signal_ref, gate_ref, cotangent_ref, gain_ref, output_ref, gate_out_ref):
    conv = unpack(conv_ref) + gain_ref[...] * signal_ref[...].astype(jnp.float32)
    output_ref[...] = (gate_ref[...].astype(jnp.float32) * conv).astype(jnp.bfloat16)
    gate_out_ref[...] = (cotangent_ref[...].astype(jnp.float32) * conv).astype(jnp.bfloat16)


def signal_grad_kernel(grad_ref, gate_ref, cotangent_ref, gain_ref, out_ref):
    gated = (cotangent_ref[...].astype(jnp.float32) * gate_ref[...].astype(jnp.float32)).astype(
        jnp.bfloat16
    )
    out_ref[...] = (unpack(grad_ref) + gain_ref[...] * gated.astype(jnp.float32)).astype(jnp.bfloat16)


def finish_call(body, packed, arrays, gain, count):
    width = gain.shape[1]
    return pl.pallas_call(
        body,
        grid=(ROWS // PACK_ROWS,),
        in_specs=[packed_spec()]
        + [row_spec(width)] * len(arrays)
        + [pl.BlockSpec((1, width), lambda i: (0, 0))],
        out_specs=[row_spec(width)] * count,
        out_shape=[jax.ShapeDtypeStruct((ROWS, width), jnp.bfloat16)] * count,
        name="finish",
    )(packed, *arrays, gain)


def exchange(blocks):
    return lax.all_to_all(blocks, "ctx", split_axis=0, concat_axis=0, tiled=True)


def per_device(signal, gate, filter_taps, skip_gain, out_cotangent):
    filters = filter_taps.shape[1] * lax.axis_size("grp")
    if (
        lax.axis_size("ctx") != CTX
        or signal.shape != (ROWS, 2 * filters)
        or filters != CTX * HALF
    ):
        return per_device_general(signal, gate, filter_taps, skip_gain, out_cotangent)
    forward, inverse = (jnp.asarray(table) for table in dense_tables())
    gain = skip_gain[None, :]
    all_taps = lax.all_gather(filter_taps, "grp", axis=1, tiled=True)
    taps_blocks = exchange(all_taps.reshape(ROWS, CTX, HALF).transpose(1, 0, 2))
    signal_blocks = exchange(pack_call(pack_kernel, [signal]))
    gated_blocks = exchange(pack_call(pack_gated_kernel, [gate, out_cotangent]))
    conv, spec, filt = conv_call(signal_blocks, taps_blocks, forward, inverse)
    conv_back = exchange(conv)
    grad, taps_grad = grad_call(gated_blocks, spec, filt, forward, inverse)
    taps_back = exchange(taps_grad).transpose(1, 0, 2).reshape(ROWS, filters)
    grad_back = exchange(grad)
    output, grad_gate = finish_call(
        outputs_kernel, conv_back, [signal, gate, out_cotangent], gain, 2
    )
    (grad_signal,) = finish_call(signal_grad_kernel, grad_back, [gate, out_cotangent], gain, 1)
    scale = 1.0 / math.sqrt(CTX * ROWS * signal.shape[1] * lax.axis_size("grp") / filters)
    grad_filter = lax.psum_scatter(taps_back, "grp", scatter_dimension=1, tiled=True)
    return (output, grad_gate, grad_signal, grad_filter.astype(jnp.float32) * scale)


def solution(mesh):
    placed = (P("ctx", "grp"), P("ctx", "grp"), P("ctx", "grp"), P("grp"), P("ctx", "grp"))
    return jax.shard_map(
        per_device,
        mesh=mesh,
        in_specs=placed,
        out_specs=(P("ctx", "grp"), P("ctx", "grp"), P("ctx", "grp"), P("ctx", "grp")),
        check_vma=False,
    )
```

```python
import math

import jax
import jax.numpy as jnp
import ml_dtypes
import numpy as np
from jax import lax
from jax.experimental import pallas as pl
from jax.experimental.pallas import tpu as pltpu
from jax.sharding import PartitionSpec as P

TWO_PI = 2.0 * math.pi


def phase_pair(first_index, second_index, length):
    products_mod = first_index[:, None] * second_index[None, :] % length
    angles = products_mod.astype(jnp.float32) * (TWO_PI / length)
    return (jnp.cos(angles), -jnp.sin(angles))


def build_tables(devices_count, block_length, table_type):
    first_length = 2 * devices_count
    cosine_first, sine_first = phase_pair(
        jnp.arange(first_length, dtype=jnp.int32),
        jnp.arange(devices_count, dtype=jnp.int32),
        first_length,
    )
    stacked_rows = jnp.concatenate([cosine_first, sine_first], axis=0).astype(table_type)
    paired_rows = jnp.stack([cosine_first, sine_first], axis=0).astype(table_type)
    cosine_rows, sine_rows = phase_pair(
        jnp.arange(block_length, dtype=jnp.int32),
        jnp.arange(block_length, dtype=jnp.int32),
        block_length,
    )
    return (stacked_rows, paired_rows, cosine_rows.astype(table_type), sine_rows.astype(table_type))


def rotate_forward(first_out, first_freq, within_block, padded):
    half_rows = first_out.shape[0] // 2
    real_part = first_out[:half_rows]
    imag_part = first_out[half_rows:]
    twiddle_real, twiddle_imag = phase_pair(first_freq, within_block, padded)
    twiddle_real = twiddle_real[:, :, None]
    twiddle_imag = twiddle_imag[:, :, None]
    return jnp.stack(
        [
            real_part * twiddle_real - imag_part * twiddle_imag,
            real_part * twiddle_imag + imag_part * twiddle_real,
        ]
    )


def second_forward(rotated, cosine_rows, sine_rows):
    with_cosine = jnp.einsum(
        "jb,pkbc->pkjc", cosine_rows, rotated, preferred_element_type=jnp.float32
    )
    with_sine = jnp.einsum("jb,pkbc->pkjc", sine_rows, rotated, preferred_element_type=jnp.float32)
    return jnp.stack([with_cosine[0] - with_sine[1], with_cosine[1] + with_sine[0]])


def inverse_front(spectra, cosine_rows, sine_rows, first_freq, padded, precise):
    precision = lax.Precision.HIGHEST if precise else None
    operand = spectra if precise else spectra.astype(jnp.bfloat16)
    with_cosine = jnp.einsum(
        "jb,pkjc->pkbc",
        cosine_rows,
        operand,
        preferred_element_type=jnp.float32,
        precision=precision,
    )
    with_sine = jnp.einsum(
        "jb,pkjc->pkbc", sine_rows, operand, preferred_element_type=jnp.float32, precision=precision
    )
    real_turned = with_cosine[0] + with_sine[1]
    imag_turned = with_cosine[1] - with_sine[0]
    twiddle_real, twiddle_imag = phase_pair(
        first_freq, jnp.arange(spectra.shape[2], dtype=jnp.int32), padded
    )
    twiddle_real = twiddle_real[:, :, None]
    twiddle_imag = twiddle_imag[:, :, None]
    rotated = jnp.stack(
        [
            real_turned * twiddle_real + imag_turned * twiddle_imag,
            imag_turned * twiddle_real - real_turned * twiddle_imag,
        ]
    )
    if precise:
        return rotated
    return rotated.astype(jnp.bfloat16)


def inverse_back(rotated, paired_rows, padded, precise):
    precision = lax.Precision.HIGHEST if precise else None
    rows_out = jnp.einsum(
        "pka,pkbc->abc",
        paired_rows,
        rotated,
        preferred_element_type=jnp.float32,
        precision=precision,
    )
    return rows_out * (1.0 / padded)


def spectral_products(spectra, filter_low, width):
    filter_wide = filter_low.astype(jnp.float32)
    filter_real = filter_wide[0]
    filter_imag = filter_wide[1]
    input_real = spectra[0, ..., :width]
    input_imag = spectra[1, ..., :width]
    grad_real = spectra[0, ..., width:]
    grad_imag = spectra[1, ..., width:]
    channel_terms = jnp.stack(
        [
            jnp.concatenate(
                [
                    input_real * filter_real - input_imag * filter_imag,
                    grad_real * filter_real + grad_imag * filter_imag,
                ],
                axis=-1,
            ),
            jnp.concatenate(
                [
                    input_real * filter_imag + input_imag * filter_real,
                    grad_imag * filter_real - grad_real * filter_imag,
                ],
                axis=-1,
            ),
        ]
    )
    filter_term = jnp.stack(
        [
            input_real * grad_real + input_imag * grad_imag,
            input_real * grad_imag - input_imag * grad_real,
        ]
    )
    return (channel_terms, filter_term)


def split_forward(values, tables, position):
    stacked_rows, paired_rows, cosine_rows, sine_rows = tables
    devices_count = lax.axis_size("ctx")
    block_length = values.shape[0]
    lane_count = block_length // devices_count
    padded = 2 * devices_count * block_length
    first_length = 2 * devices_count
    first_out = jnp.einsum(
        "ka,abc->kbc",
        stacked_rows,
        lax.all_to_all(values[None], "ctx", split_axis=1, concat_axis=0, tiled=True),
        preferred_element_type=jnp.float32,
    )
    within_block = position * lane_count + jnp.arange(lane_count, dtype=jnp.int32)
    rotated = rotate_forward(
        first_out, jnp.arange(first_length, dtype=jnp.int32), within_block, padded
    ).astype(jnp.bfloat16)
    return second_forward(
        lax.all_to_all(rotated, "ctx", split_axis=1, concat_axis=2, tiled=True),
        cosine_rows,
        sine_rows,
    )


def split_inverse(spectra, tables, position, precise):
    stacked_rows, paired_rows, cosine_rows, sine_rows = tables
    devices_count = lax.axis_size("ctx")
    freq_count = spectra.shape[1]
    padded = 2 * devices_count * spectra.shape[2]
    first_freq = position * freq_count + jnp.arange(freq_count, dtype=jnp.int32)
    rotated = inverse_front(spectra, cosine_rows, sine_rows, first_freq, padded, precise)
    if precise:
        last_rows_out = inverse_back(
            lax.all_to_all(
                rotated.astype(jnp.bfloat16), "ctx", split_axis=2, concat_axis=1, tiled=True
            ).astype(rotated.dtype),
            paired_rows,
            padded,
            True,
        )
        result = lax.all_to_all(
            last_rows_out.astype(jnp.bfloat16), "ctx", split_axis=0, concat_axis=1, tiled=True
        ).astype(last_rows_out.dtype)
    else:
        rows_out = inverse_back(
            lax.all_to_all(rotated, "ctx", split_axis=2, concat_axis=1, tiled=True),
            paired_rows,
            padded,
            False,
        )
        result = lax.all_to_all(
            rows_out.astype(jnp.bfloat16), "ctx", split_axis=0, concat_axis=1, tiled=True
        ).astype(rows_out.dtype)
    return result[0]


def per_device_general(signal, gate, filter_taps, skip_gain, out_cotangent):
    devices_count = lax.axis_size("ctx")
    group_count = lax.axis_size("grp")
    block_length = signal.shape[0]
    local_channels = signal.shape[1]
    filters = filter_taps.shape[1] * group_count
    repeats = local_channels // filters
    position = lax.axis_index("ctx")
    coarse_tables = build_tables(devices_count, block_length, jnp.bfloat16)
    exact_tables = build_tables(devices_count, block_length, jnp.float32)
    gated = (out_cotangent.astype(jnp.float32) * gate.astype(jnp.float32)).astype(jnp.bfloat16)
    gain_wide = skip_gain[None, :]
    all_filters = lax.all_gather(filter_taps, "grp", axis=1, tiled=True)
    filter_low = lax.optimization_barrier(
        split_forward(all_filters, coarse_tables, position).astype(jnp.bfloat16)
    )
    filter_totals = jnp.zeros((2, 2, block_length, filters), jnp.float32)
    conv_blocks = []
    grad_blocks = []
    for block_index in range(repeats):
        lower = block_index * filters
        columns = jnp.concatenate(
            [signal[:, lower : lower + filters], gated[:, lower : lower + filters]], axis=1
        )
        spectra = split_forward(columns, coarse_tables, position)
        channel_terms, filter_term = spectral_products(spectra, filter_low, filters)
        filter_totals = filter_totals + filter_term
        signal_back = split_inverse(channel_terms, coarse_tables, position, False)
        conv_blocks.append(signal_back[:, :filters])
        grad_blocks.append(signal_back[:, filters:])
    conv_part = jnp.concatenate(conv_blocks, axis=1)
    grad_conv = jnp.concatenate(grad_blocks, axis=1)
    filter_back = split_inverse(filter_totals, exact_tables, position, True)
    grad_filter = lax.psum_scatter(
        filter_back.astype(jnp.bfloat16), "grp", scatter_dimension=1, tiled=True
    ).astype(jnp.float32)
    conv_part = conv_part + gain_wide * signal.astype(jnp.float32)
    output = (gate.astype(jnp.float32) * conv_part).astype(jnp.bfloat16)
    grad_gate = (out_cotangent.astype(jnp.float32) * conv_part).astype(jnp.bfloat16)
    grad_signal = (grad_conv + gain_wide * gated.astype(jnp.float32)).astype(jnp.bfloat16)
    scale = 1.0 / math.sqrt(devices_count * block_length * local_channels * group_count / filters)
    return (output, grad_gate, grad_signal, grad_filter * scale)


CTX = 8
FIRST = 16
ROWS = 512
LANES = 128
HALF = 64
STRIP = 16
PER_STEP = 4


def low(values):
    return np.asarray(values, np.float32).astype(ml_dtypes.bfloat16)


def first_coefficients():
    index = np.arange(FIRST)
    angles = (index[:, None] * index[None, :] % FIRST).astype(np.float32) * np.float32(TWO_PI / FIRST)
    return (
        low(np.round(np.cos(angles), 7)).astype(np.float64),
        low(np.round(np.sin(angles), 7)).astype(np.float64),
    )


def dense_tables():
    index = np.arange(ROWS)
    angles = (index[:, None] * index[None, :] % ROWS).astype(np.float32) * np.float32(TWO_PI / ROWS)
    table = low(np.concatenate([np.cos(angles), -np.sin(angles)], axis=1))
    turn = index * (TWO_PI / (FIRST * ROWS))
    turns = np.stack([np.cos(turn), -np.sin(turn)])[:, :, None]
    return table, np.broadcast_to(turns, (2, ROWS, LANES)).astype(np.float32)


COS, SIN = first_coefficients()


def scaled_sum(terms):
    total = None
    for coefficient, value in terms:
        coefficient = float(coefficient)
        if abs(coefficient) < 1e-6:
            continue
        if total is None:
            total = value if coefficient == 1.0 else value * coefficient
        elif coefficient == 1.0:
            total = total + value
        elif coefficient == -1.0:
            total = total - value
        else:
            total = total + value * coefficient
    return total


def lower_half(shape):
    return lax.broadcasted_iota(jnp.int32, shape, len(shape) - 1) < HALF


def swap(values):
    return pltpu.roll(values, HALF, axis=1)


def times_i(values, sign):
    return swap(values) * sign


def forward_first(blocks, sign):
    plus = {a: blocks[a] + blocks[8 - a] for a in (1, 2, 3)}
    minus = {a: blocks[a] - blocks[8 - a] for a in (1, 2, 3)}
    results = [None] * FIRST
    for k in range(9):
        if k % 2 == 0:
            real = scaled_sum(
                [(1.0, blocks[0]), (COS[k, 4], blocks[4])] + [(COS[k, a], plus[a]) for a in (1, 2, 3)]
            )
            turned = scaled_sum([(-SIN[k, a], minus[a]) for a in (1, 2, 3)])
        else:
            real = scaled_sum([(1.0, blocks[0])] + [(COS[k, a], minus[a]) for a in (1, 2, 3)])
            turned = scaled_sum([(-SIN[k, 4], blocks[4])] + [(-SIN[k, a], plus[a]) for a in (1, 2, 3)])
        real_turned = times_i(real, sign)
        if turned is None:
            results[k] = (real, real_turned)
            continue
        twice = times_i(turned, sign)
        results[k] = (real + twice, real_turned - turned)
        results[FIRST - k] = (real - twice, real_turned + turned)
    return results


def inverse_last(parts, sign):
    even = {k: parts[k] + parts[FIRST - k] for k in range(1, 8)}
    odd = {k: parts[k] - parts[FIRST - k] for k in range(1, 8)}
    results = [None] * CTX
    for a in range(5):
        flip = 1.0 if a % 2 == 0 else -1.0
        real_even = scaled_sum(
            [(1.0, parts[0]), (flip, parts[8])] + [(COS[k, a], even[k]) for k in (2, 4, 6)]
        )
        real_odd = scaled_sum([(COS[k, a], even[k]) for k in (1, 3, 5, 7)])
        turn_even = scaled_sum([(SIN[k, a], odd[k]) for k in (2, 4, 6)])
        turn_odd = scaled_sum([(SIN[k, a], odd[k]) for k in (1, 3, 5, 7)])
        real = real_even if real_odd is None else real_even + real_odd
        if a == 0:
            results[0] = real
            continue
        if a == 4:
            results[4] = real + times_i(turn_odd, sign)
            continue
        results[a] = real + times_i(turn_even + turn_odd, sign)
        results[8 - a] = (real_even - real_odd) + times_i(turn_odd - turn_even, sign)
    return results


def signs():
    return jnp.where(lower_half((1, LANES)), -1.0, 1.0).astype(jnp.float32)


def next_turn(turn, unit):
    return (turn[0] * unit[0] - turn[1] * unit[1], turn[0] * unit[1] + turn[1] * unit[0])


def stage_one(load, turns_ref, stacked_ref, lane_start):
    sign = signs()

    @pl.loop(0, ROWS // STRIP)
    def _(strip):
        rows = pl.multiple_of(strip * STRIP, STRIP)
        blocks = [load(a, pl.ds(rows, STRIP)) for a in range(CTX)]
        unit = (turns_ref[0, pl.ds(rows, STRIP), :], turns_ref[1, pl.ds(rows, STRIP), :])
        lanes = slice(lane_start, lane_start + LANES)
        turn = None
        for k, (values, turned) in enumerate(forward_first(blocks, sign)):
            if k > 0:
                turn = unit if turn is None else next_turn(turn, unit)
                values, turned = (
                    values * turn[0] + turned * turn[1],
                    turned * turn[0] - values * turn[1],
                )
            stacked_ref[k, pl.ds(rows, STRIP), lanes] = values.astype(jnp.bfloat16)
            stacked_ref[k, pl.ds(ROWS + rows, STRIP), lanes] = turned.astype(jnp.bfloat16)


def last_stage(half_ref, turns_ref, lane_start, store):
    sign = signs()

    @pl.loop(0, ROWS // STRIP)
    def _(strip):
        rows = pl.multiple_of(strip * STRIP, STRIP)
        unit = (turns_ref[0, pl.ds(rows, STRIP), :], turns_ref[1, pl.ds(rows, STRIP), :])
        turn = (1.0 / (FIRST * ROWS), 0.0)
        parts = []
        for k in range(FIRST):
            part = half_ref[k, pl.ds(rows, STRIP), lane_start : lane_start + LANES].astype(
                jnp.float32
            )
            if k == 0:
                parts.append(part * turn[0])
                continue
            turn = (turn[0] * unit[0], turn[0] * unit[1]) if k == 1 else next_turn(turn, unit)
            parts.append(part * turn[0] - times_i(part, sign) * turn[1])
        for a, values in enumerate(inverse_last(parts, sign)):
            store(a, pl.ds(rows, STRIP), values)


def conv_kernel(signal_ref, taps_ref, table_ref, turns_ref, conv_ref, spec_ref, filt_ref,
                stacked, half):
    k = pl.program_id(0)

    @pl.when(k == 0)
    def _():
        stage_one(lambda a, rows: signal_ref[a, rows, :].astype(jnp.float32), turns_ref, stacked, 0)

        def load_taps(a, rows):
            values = taps_ref[a, rows, :].astype(jnp.float32)
            return jnp.concatenate([values, jnp.zeros_like(values)], axis=1)

        stage_one(load_taps, turns_ref, stacked, LANES)

    sign = signs()
    all_spectra = [
        jnp.dot(table_ref[...], stacked[k * PER_STEP + sub], preferred_element_type=jnp.float32)
        for sub in range(PER_STEP)
    ]
    for sub, spectra in enumerate(all_spectra):
        signal_spec = spectra[:, :LANES]
        filter_low = spectra[:, LANES:].astype(jnp.bfloat16)
        spec_ref[sub] = signal_spec.astype(jnp.bfloat16)
        filt_ref[sub] = filter_low
        filter_wide = filter_low.astype(jnp.float32)
        swapped = swap(filter_wide)
        first_half = lower_half((ROWS, LANES))
        filter_real = jnp.where(first_half, filter_wide, swapped)
        filter_imag = jnp.where(first_half, swapped, filter_wide)
        product = signal_spec * filter_real + times_i(signal_spec, sign) * filter_imag
        operand = jnp.concatenate([product, times_i(product, -sign)], axis=0).astype(jnp.bfloat16)
        half[k * PER_STEP + sub] = jnp.dot(table_ref[...], operand, preferred_element_type=jnp.float32).astype(
            jnp.bfloat16
        )

    @pl.when(k == FIRST // PER_STEP - 1)
    def _():
        def store(a, rows, values):
            conv_ref[a, rows, :] = values.astype(jnp.bfloat16)

        last_stage(half, turns_ref, 0, store)


def grad_kernel(gated_ref, spec_ref, filt_ref, table_ref, turns_ref, grad_ref, taps_ref,
                stacked, half):
    k = pl.program_id(0)

    @pl.when(k == 0)
    def _():
        stage_one(lambda a, rows: gated_ref[a, rows, :].astype(jnp.float32), turns_ref, stacked, 0)

    sign = signs()
    all_spectra = [
        jnp.dot(table_ref[...], stacked[k * PER_STEP + sub], preferred_element_type=jnp.float32)
        for sub in range(PER_STEP)
    ]
    for sub, spectra in enumerate(all_spectra):
        turned = times_i(spectra, sign)
        first_half = lower_half((ROWS, LANES))

        def split(values):
            swapped = swap(values)
            return jnp.where(first_half, values, swapped), jnp.where(first_half, swapped, values)

        filter_real, filter_imag = split(filt_ref[sub].astype(jnp.float32))
        signal_real, signal_imag = split(spec_ref[sub].astype(jnp.float32))
        back = spectra * filter_real - turned * filter_imag
        cross = spectra * signal_real - turned * signal_imag
        operand = jnp.concatenate(
            [
                jnp.concatenate([back, cross], axis=1),
                jnp.concatenate([times_i(back, -sign), times_i(cross, -sign)], axis=1),
            ],
            axis=0,
        ).astype(jnp.bfloat16)
        half[k * PER_STEP + sub] = jnp.dot(table_ref[...], operand, preferred_element_type=jnp.float32).astype(
            jnp.bfloat16
        )

    @pl.when(k == FIRST // PER_STEP - 1)
    def _():
        def store(a, rows, values):
            grad_ref[a, rows, :] = values.astype(jnp.bfloat16)

        def store_taps(a, rows, values):
            taps_ref[a, rows, :] = values[:, :HALF].astype(jnp.bfloat16)

        last_stage(half, turns_ref, 0, store)
        last_stage(half, turns_ref, LANES, store_taps)


def whole_spec(shape):
    return pl.BlockSpec(shape, lambda k: (0,) * len(shape))


def each_spec(shape):
    return pl.BlockSpec((PER_STEP,) + shape, lambda k: (k,) + (0,) * len(shape))


TABLE_SPECS = [whole_spec((ROWS, 2 * ROWS)), whole_spec((2, ROWS, LANES))]
PARAMS = pltpu.CompilerParams(vmem_limit_bytes=56 * 1024 * 1024)
WORK = 2 * FIRST * ROWS * 2 * ROWS * 2 * LANES * 2
COST = pl.CostEstimate(flops=WORK, bytes_accessed=60 * 1024 * 1024, transcendentals=0)


def conv_call(signal_blocks, taps_blocks, table, turns):
    block = (CTX, ROWS, LANES)
    return pl.pallas_call(
        conv_kernel,
        grid=(FIRST // PER_STEP,),
        in_specs=[whole_spec(block), whole_spec((CTX, ROWS, HALF))] + TABLE_SPECS,
        out_specs=[whole_spec(block), each_spec((ROWS, LANES)), each_spec((ROWS, LANES))],
        out_shape=[
            jax.ShapeDtypeStruct(block, jnp.bfloat16),
            jax.ShapeDtypeStruct((FIRST, ROWS, LANES), jnp.bfloat16),
            jax.ShapeDtypeStruct((FIRST, ROWS, LANES), jnp.bfloat16),
        ],
        scratch_shapes=[
            pltpu.VMEM((FIRST, 2 * ROWS, 2 * LANES), jnp.bfloat16),
            pltpu.VMEM((FIRST, ROWS, LANES), jnp.bfloat16),
        ],
        compiler_params=PARAMS,
        cost_estimate=COST,
        name="conv_part",
    )(signal_blocks, taps_blocks, table, turns)


def grad_call(gated_blocks, spec, filt, table, turns):
    block = (CTX, ROWS, LANES)
    return pl.pallas_call(
        grad_kernel,
        grid=(FIRST // PER_STEP,),
        in_specs=[
            whole_spec(block),
            each_spec((ROWS, LANES)),
            each_spec((ROWS, LANES)),
        ]
        + TABLE_SPECS,
        out_specs=[whole_spec(block), whole_spec((CTX, ROWS, HALF))],
        out_shape=[
            jax.ShapeDtypeStruct(block, jnp.bfloat16),
            jax.ShapeDtypeStruct((CTX, ROWS, HALF), jnp.bfloat16),
        ],
        scratch_shapes=[
            pltpu.VMEM((FIRST, 2 * ROWS, LANES), jnp.bfloat16),
            pltpu.VMEM((FIRST, ROWS, 2 * LANES), jnp.bfloat16),
        ],
        compiler_params=PARAMS,
        cost_estimate=COST,
        name="grad_part",
    )(gated_blocks, spec, filt, table, turns)


def pack_pair(values, p):
    offset = CTX * HALF
    return jnp.concatenate(
        [values[:, HALF * p : HALF * p + HALF], values[:, offset + HALF * p : offset + HALF * p + HALF]],
        axis=1,
    )


def pack_kernel(signal_ref, packed_ref):
    values = signal_ref[...].astype(jnp.float32)
    for p in range(CTX):
        packed_ref[p] = pack_pair(values, p).astype(jnp.bfloat16)


def pack_gated_kernel(gate_ref, cotangent_ref, packed_ref):
    values = cotangent_ref[...].astype(jnp.float32) * gate_ref[...].astype(jnp.float32)
    for p in range(CTX):
        packed_ref[p] = pack_pair(values, p).astype(jnp.bfloat16)


PACK_ROWS = 128


def row_spec(width):
    return pl.BlockSpec((PACK_ROWS, width), lambda i: (i, 0))


def packed_spec():
    return pl.BlockSpec((CTX, PACK_ROWS, LANES), lambda i: (0, i, 0))


def pack_call(body, arrays):
    return pl.pallas_call(
        body,
        grid=(ROWS // PACK_ROWS,),
        in_specs=[row_spec(array.shape[1]) for array in arrays],
        out_specs=packed_spec(),
        out_shape=jax.ShapeDtypeStruct((CTX, ROWS, LANES), jnp.bfloat16),
        name="pack",
    )(*arrays)


def unpack(ref):
    blocks = [ref[p].astype(jnp.float32) for p in range(CTX)]
    return jnp.concatenate(
        [block[:, :HALF] for block in blocks] + [block[:, HALF:] for block in blocks], axis=1
    )


def outputs_kernel(conv_ref, signal_ref, gate_ref, cotangent_ref, gain_ref, output_ref, gate_out_ref):
    conv = unpack(conv_ref) + gain_ref[...] * signal_ref[...].astype(jnp.float32)
    output_ref[...] = (gate_ref[...].astype(jnp.float32) * conv).astype(jnp.bfloat16)
    gate_out_ref[...] = (cotangent_ref[...].astype(jnp.float32) * conv).astype(jnp.bfloat16)


def signal_grad_kernel(grad_ref, gate_ref, cotangent_ref, gain_ref, out_ref):
    gated = (cotangent_ref[...].astype(jnp.float32) * gate_ref[...].astype(jnp.float32)).astype(
        jnp.bfloat16
    )
    out_ref[...] = (unpack(grad_ref) + gain_ref[...] * gated.astype(jnp.float32)).astype(jnp.bfloat16)


def finish_call(body, packed, arrays, gain, count):
    width = gain.shape[1]
    return pl.pallas_call(
        body,
        grid=(ROWS // PACK_ROWS,),
        in_specs=[packed_spec()]
        + [row_spec(width)] * len(arrays)
        + [pl.BlockSpec((1, width), lambda i: (0, 0))],
        out_specs=[row_spec(width)] * count,
        out_shape=[jax.ShapeDtypeStruct((ROWS, width), jnp.bfloat16)] * count,
        name="finish",
    )(packed, *arrays, gain)


def exchange(blocks):
    return lax.all_to_all(blocks, "ctx", split_axis=0, concat_axis=0, tiled=True)


def per_device(signal, gate, filter_taps, skip_gain, out_cotangent):
    filters = filter_taps.shape[1] * lax.axis_size("grp")
    if (
        lax.axis_size("ctx") != CTX
        or signal.shape != (ROWS, 2 * filters)
        or filters != CTX * HALF
    ):
        return per_device_general(signal, gate, filter_taps, skip_gain, out_cotangent)
    table, turns = (jnp.asarray(table) for table in dense_tables())
    gain = skip_gain[None, :]
    all_taps = lax.all_gather(filter_taps, "grp", axis=1, tiled=True)
    taps_blocks = exchange(all_taps.reshape(ROWS, CTX, HALF).transpose(1, 0, 2))
    signal_blocks = exchange(pack_call(pack_kernel, [signal]))
    gated_blocks = exchange(pack_call(pack_gated_kernel, [gate, out_cotangent]))
    conv, spec, filt = conv_call(signal_blocks, taps_blocks, table, turns)
    conv_back = exchange(conv)
    grad, taps_grad = grad_call(gated_blocks, spec, filt, table, turns)
    grad, taps_grad, conv_back = lax.optimization_barrier((grad, taps_grad, conv_back))
    taps_back = exchange(taps_grad).transpose(1, 0, 2).reshape(ROWS, filters)
    grad_back = exchange(grad)
    output, grad_gate = finish_call(
        outputs_kernel, conv_back, [signal, gate, out_cotangent], gain, 2
    )
    (grad_signal,) = finish_call(signal_grad_kernel, grad_back, [gate, out_cotangent], gain, 1)
    scale = 1.0 / math.sqrt(CTX * ROWS * signal.shape[1] * lax.axis_size("grp") / filters)
    grad_filter = lax.psum_scatter(taps_back, "grp", scatter_dimension=1, tiled=True)
    return (output, grad_gate, grad_signal, grad_filter.astype(jnp.float32) * scale)


def solution(mesh):
    placed = (P("ctx", "grp"), P("ctx", "grp"), P("ctx", "grp"), P("grp"), P("ctx", "grp"))
    return jax.shard_map(
        per_device,
        mesh=mesh,
        in_specs=placed,
        out_specs=(P("ctx", "grp"), P("ctx", "grp"), P("ctx", "grp"), P("ctx", "grp")),
        check_vma=False,
    )
```

```python
import math

import jax
import jax.numpy as jnp
import ml_dtypes
import numpy as np
from jax import lax
from jax.experimental import pallas as pl
from jax.experimental.pallas import tpu as pltpu
from jax.sharding import PartitionSpec as P

TWO_PI = 2.0 * math.pi


def phase_pair(first_index, second_index, length):
    products_mod = first_index[:, None] * second_index[None, :] % length
    angles = products_mod.astype(jnp.float32) * (TWO_PI / length)
    return (jnp.cos(angles), -jnp.sin(angles))


def build_tables(devices_count, block_length, table_type):
    first_length = 2 * devices_count
    cosine_first, sine_first = phase_pair(
        jnp.arange(first_length, dtype=jnp.int32),
        jnp.arange(devices_count, dtype=jnp.int32),
        first_length,
    )
    stacked_rows = jnp.concatenate([cosine_first, sine_first], axis=0).astype(table_type)
    paired_rows = jnp.stack([cosine_first, sine_first], axis=0).astype(table_type)
    cosine_rows, sine_rows = phase_pair(
        jnp.arange(block_length, dtype=jnp.int32),
        jnp.arange(block_length, dtype=jnp.int32),
        block_length,
    )
    return (stacked_rows, paired_rows, cosine_rows.astype(table_type), sine_rows.astype(table_type))


def rotate_forward(first_out, first_freq, within_block, padded):
    half_rows = first_out.shape[0] // 2
    real_part = first_out[:half_rows]
    imag_part = first_out[half_rows:]
    twiddle_real, twiddle_imag = phase_pair(first_freq, within_block, padded)
    twiddle_real = twiddle_real[:, :, None]
    twiddle_imag = twiddle_imag[:, :, None]
    return jnp.stack(
        [
            real_part * twiddle_real - imag_part * twiddle_imag,
            real_part * twiddle_imag + imag_part * twiddle_real,
        ]
    )


def second_forward(rotated, cosine_rows, sine_rows):
    with_cosine = jnp.einsum(
        "jb,pkbc->pkjc", cosine_rows, rotated, preferred_element_type=jnp.float32
    )
    with_sine = jnp.einsum("jb,pkbc->pkjc", sine_rows, rotated, preferred_element_type=jnp.float32)
    return jnp.stack([with_cosine[0] - with_sine[1], with_cosine[1] + with_sine[0]])


def inverse_front(spectra, cosine_rows, sine_rows, first_freq, padded, precise):
    precision = lax.Precision.HIGHEST if precise else None
    operand = spectra if precise else spectra.astype(jnp.bfloat16)
    with_cosine = jnp.einsum(
        "jb,pkjc->pkbc",
        cosine_rows,
        operand,
        preferred_element_type=jnp.float32,
        precision=precision,
    )
    with_sine = jnp.einsum(
        "jb,pkjc->pkbc", sine_rows, operand, preferred_element_type=jnp.float32, precision=precision
    )
    real_turned = with_cosine[0] + with_sine[1]
    imag_turned = with_cosine[1] - with_sine[0]
    twiddle_real, twiddle_imag = phase_pair(
        first_freq, jnp.arange(spectra.shape[2], dtype=jnp.int32), padded
    )
    twiddle_real = twiddle_real[:, :, None]
    twiddle_imag = twiddle_imag[:, :, None]
    rotated = jnp.stack(
        [
            real_turned * twiddle_real + imag_turned * twiddle_imag,
            imag_turned * twiddle_real - real_turned * twiddle_imag,
        ]
    )
    if precise:
        return rotated
    return rotated.astype(jnp.bfloat16)


def inverse_back(rotated, paired_rows, padded, precise):
    precision = lax.Precision.HIGHEST if precise else None
    rows_out = jnp.einsum(
        "pka,pkbc->abc",
        paired_rows,
        rotated,
        preferred_element_type=jnp.float32,
        precision=precision,
    )
    return rows_out * (1.0 / padded)


def spectral_products(spectra, filter_low, width):
    filter_wide = filter_low.astype(jnp.float32)
    filter_real = filter_wide[0]
    filter_imag = filter_wide[1]
    input_real = spectra[0, ..., :width]
    input_imag = spectra[1, ..., :width]
    grad_real = spectra[0, ..., width:]
    grad_imag = spectra[1, ..., width:]
    channel_terms = jnp.stack(
        [
            jnp.concatenate(
                [
                    input_real * filter_real - input_imag * filter_imag,
                    grad_real * filter_real + grad_imag * filter_imag,
                ],
                axis=-1,
            ),
            jnp.concatenate(
                [
                    input_real * filter_imag + input_imag * filter_real,
                    grad_imag * filter_real - grad_real * filter_imag,
                ],
                axis=-1,
            ),
        ]
    )
    filter_term = jnp.stack(
        [
            input_real * grad_real + input_imag * grad_imag,
            input_real * grad_imag - input_imag * grad_real,
        ]
    )
    return (channel_terms, filter_term)


def split_forward(values, tables, position):
    stacked_rows, paired_rows, cosine_rows, sine_rows = tables
    devices_count = lax.axis_size("ctx")
    block_length = values.shape[0]
    lane_count = block_length // devices_count
    padded = 2 * devices_count * block_length
    first_length = 2 * devices_count
    first_out = jnp.einsum(
        "ka,abc->kbc",
        stacked_rows,
        lax.all_to_all(values[None], "ctx", split_axis=1, concat_axis=0, tiled=True),
        preferred_element_type=jnp.float32,
    )
    within_block = position * lane_count + jnp.arange(lane_count, dtype=jnp.int32)
    rotated = rotate_forward(
        first_out, jnp.arange(first_length, dtype=jnp.int32), within_block, padded
    ).astype(jnp.bfloat16)
    return second_forward(
        lax.all_to_all(rotated, "ctx", split_axis=1, concat_axis=2, tiled=True),
        cosine_rows,
        sine_rows,
    )


def split_inverse(spectra, tables, position, precise):
    stacked_rows, paired_rows, cosine_rows, sine_rows = tables
    devices_count = lax.axis_size("ctx")
    freq_count = spectra.shape[1]
    padded = 2 * devices_count * spectra.shape[2]
    first_freq = position * freq_count + jnp.arange(freq_count, dtype=jnp.int32)
    rotated = inverse_front(spectra, cosine_rows, sine_rows, first_freq, padded, precise)
    if precise:
        last_rows_out = inverse_back(
            lax.all_to_all(
                rotated.astype(jnp.bfloat16), "ctx", split_axis=2, concat_axis=1, tiled=True
            ).astype(rotated.dtype),
            paired_rows,
            padded,
            True,
        )
        result = lax.all_to_all(
            last_rows_out.astype(jnp.bfloat16), "ctx", split_axis=0, concat_axis=1, tiled=True
        ).astype(last_rows_out.dtype)
    else:
        rows_out = inverse_back(
            lax.all_to_all(rotated, "ctx", split_axis=2, concat_axis=1, tiled=True),
            paired_rows,
            padded,
            False,
        )
        result = lax.all_to_all(
            rows_out.astype(jnp.bfloat16), "ctx", split_axis=0, concat_axis=1, tiled=True
        ).astype(rows_out.dtype)
    return result[0]


def per_device_general(signal, gate, filter_taps, skip_gain, out_cotangent):
    devices_count = lax.axis_size("ctx")
    group_count = lax.axis_size("grp")
    block_length = signal.shape[0]
    local_channels = signal.shape[1]
    filters = filter_taps.shape[1] * group_count
    repeats = local_channels // filters
    position = lax.axis_index("ctx")
    coarse_tables = build_tables(devices_count, block_length, jnp.bfloat16)
    exact_tables = build_tables(devices_count, block_length, jnp.float32)
    gated = (out_cotangent.astype(jnp.float32) * gate.astype(jnp.float32)).astype(jnp.bfloat16)
    gain_wide = skip_gain[None, :]
    all_filters = lax.all_gather(filter_taps, "grp", axis=1, tiled=True)
    filter_low = lax.optimization_barrier(
        split_forward(all_filters, coarse_tables, position).astype(jnp.bfloat16)
    )
    filter_totals = jnp.zeros((2, 2, block_length, filters), jnp.float32)
    conv_blocks = []
    grad_blocks = []
    for block_index in range(repeats):
        lower = block_index * filters
        columns = jnp.concatenate(
            [signal[:, lower : lower + filters], gated[:, lower : lower + filters]], axis=1
        )
        spectra = split_forward(columns, coarse_tables, position)
        channel_terms, filter_term = spectral_products(spectra, filter_low, filters)
        filter_totals = filter_totals + filter_term
        signal_back = split_inverse(channel_terms, coarse_tables, position, False)
        conv_blocks.append(signal_back[:, :filters])
        grad_blocks.append(signal_back[:, filters:])
    conv_part = jnp.concatenate(conv_blocks, axis=1)
    grad_conv = jnp.concatenate(grad_blocks, axis=1)
    filter_back = split_inverse(filter_totals, exact_tables, position, True)
    grad_filter = lax.psum_scatter(
        filter_back.astype(jnp.bfloat16), "grp", scatter_dimension=1, tiled=True
    ).astype(jnp.float32)
    conv_part = conv_part + gain_wide * signal.astype(jnp.float32)
    output = (gate.astype(jnp.float32) * conv_part).astype(jnp.bfloat16)
    grad_gate = (out_cotangent.astype(jnp.float32) * conv_part).astype(jnp.bfloat16)
    grad_signal = (grad_conv + gain_wide * gated.astype(jnp.float32)).astype(jnp.bfloat16)
    scale = 1.0 / math.sqrt(devices_count * block_length * local_channels * group_count / filters)
    return (output, grad_gate, grad_signal, grad_filter * scale)


CTX = 8
FIRST = 16
ROWS = 512
LANES = 128
HALF = 64
STRIP = 16
PER_STEP = 4


def low(values):
    return np.asarray(values, np.float32).astype(ml_dtypes.bfloat16)


def first_coefficients():
    index = np.arange(FIRST)
    angles = (index[:, None] * index[None, :] % FIRST).astype(np.float32) * np.float32(TWO_PI / FIRST)
    return (
        low(np.round(np.cos(angles), 7)).astype(np.float64),
        low(np.round(np.sin(angles), 7)).astype(np.float64),
    )


def dense_tables():
    index = np.arange(ROWS)
    angles = (index[:, None] * index[None, :] % ROWS).astype(np.float32) * np.float32(TWO_PI / ROWS)
    table = low(np.concatenate([np.cos(angles), -np.sin(angles)], axis=1))
    turn = index * (TWO_PI / (FIRST * ROWS))
    turns = np.stack([np.cos(turn), -np.sin(turn)])[:, :, None]
    return table, np.broadcast_to(turns, (2, ROWS, LANES)).astype(np.float32)


COS, SIN = first_coefficients()


def scaled_sum(terms):
    total = None
    for coefficient, value in terms:
        coefficient = float(coefficient)
        if abs(coefficient) < 1e-6:
            continue
        if total is None:
            total = value if coefficient == 1.0 else value * coefficient
        elif coefficient == 1.0:
            total = total + value
        elif coefficient == -1.0:
            total = total - value
        else:
            total = total + value * coefficient
    return total


def lower_half(shape):
    return lax.broadcasted_iota(jnp.int32, shape, len(shape) - 1) < HALF


def swap(values):
    return pltpu.roll(values, HALF, axis=1)


def times_i(values, sign):
    return swap(values) * sign


def forward_first(blocks, sign):
    plus = {a: blocks[a] + blocks[8 - a] for a in (1, 2, 3)}
    minus = {a: blocks[a] - blocks[8 - a] for a in (1, 2, 3)}
    results = [None] * FIRST
    for k in range(9):
        if k % 2 == 0:
            real = scaled_sum(
                [(1.0, blocks[0]), (COS[k, 4], blocks[4])] + [(COS[k, a], plus[a]) for a in (1, 2, 3)]
            )
            turned = scaled_sum([(-SIN[k, a], minus[a]) for a in (1, 2, 3)])
        else:
            real = scaled_sum([(1.0, blocks[0])] + [(COS[k, a], minus[a]) for a in (1, 2, 3)])
            turned = scaled_sum([(-SIN[k, 4], blocks[4])] + [(-SIN[k, a], plus[a]) for a in (1, 2, 3)])
        real_turned = times_i(real, sign)
        if turned is None:
            results[k] = (real, real_turned)
            continue
        twice = times_i(turned, sign)
        results[k] = (real + twice, real_turned - turned)
        results[FIRST - k] = (real - twice, real_turned + turned)
    return results


def inverse_last(parts, sign):
    even = {k: parts[k] + parts[FIRST - k] for k in range(1, 8)}
    odd = {k: parts[k] - parts[FIRST - k] for k in range(1, 8)}
    results = [None] * CTX
    for a in range(5):
        flip = 1.0 if a % 2 == 0 else -1.0
        real_even = scaled_sum(
            [(1.0, parts[0]), (flip, parts[8])] + [(COS[k, a], even[k]) for k in (2, 4, 6)]
        )
        real_odd = scaled_sum([(COS[k, a], even[k]) for k in (1, 3, 5, 7)])
        turn_even = scaled_sum([(SIN[k, a], odd[k]) for k in (2, 4, 6)])
        turn_odd = scaled_sum([(SIN[k, a], odd[k]) for k in (1, 3, 5, 7)])
        real = real_even if real_odd is None else real_even + real_odd
        if a == 0:
            results[0] = real
            continue
        if a == 4:
            results[4] = real + times_i(turn_odd, sign)
            continue
        results[a] = real + times_i(turn_even + turn_odd, sign)
        results[8 - a] = (real_even - real_odd) + times_i(turn_odd - turn_even, sign)
    return results


def signs():
    return jnp.where(lower_half((1, LANES)), -1.0, 1.0).astype(jnp.float32)


def next_turn(turn, unit):
    return (turn[0] * unit[0] - turn[1] * unit[1], turn[0] * unit[1] + turn[1] * unit[0])


def stage_one(load, turns_ref, stacked_ref, lane_start):
    sign = signs()

    @pl.loop(0, ROWS // STRIP)
    def _(strip):
        rows = pl.multiple_of(strip * STRIP, STRIP)
        blocks = [load(a, pl.ds(rows, STRIP)) for a in range(CTX)]
        unit = (turns_ref[0, pl.ds(rows, STRIP), :], turns_ref[1, pl.ds(rows, STRIP), :])
        lanes = slice(lane_start, lane_start + LANES)
        turn = None
        for k, (values, turned) in enumerate(forward_first(blocks, sign)):
            if k > 0:
                turn = unit if turn is None else next_turn(turn, unit)
                values, turned = (
                    values * turn[0] + turned * turn[1],
                    turned * turn[0] - values * turn[1],
                )
            stacked_ref[k, pl.ds(rows, STRIP), lanes] = values.astype(jnp.bfloat16)
            stacked_ref[k, pl.ds(ROWS + rows, STRIP), lanes] = turned.astype(jnp.bfloat16)


def last_stage(half_ref, turns_ref, lane_start, store):
    sign = signs()

    @pl.loop(0, ROWS // STRIP)
    def _(strip):
        rows = pl.multiple_of(strip * STRIP, STRIP)
        unit = (turns_ref[0, pl.ds(rows, STRIP), :], turns_ref[1, pl.ds(rows, STRIP), :])
        turn = (1.0 / (FIRST * ROWS), 0.0)
        parts = []
        for k in range(FIRST):
            part = half_ref[k, pl.ds(rows, STRIP), lane_start : lane_start + LANES].astype(
                jnp.float32
            )
            if k == 0:
                parts.append(part * turn[0])
                continue
            turn = (turn[0] * unit[0], turn[0] * unit[1]) if k == 1 else next_turn(turn, unit)
            parts.append(part * turn[0] - times_i(part, sign) * turn[1])
        for a, values in enumerate(inverse_last(parts, sign)):
            store(a, pl.ds(rows, STRIP), values)


def conv_kernel(signal_ref, taps_ref, table_ref, turns_ref, conv_ref, spec_ref, filt_ref,
                stacked, half):
    k = pl.program_id(0)

    @pl.when(k == 0)
    def _():
        stage_one(lambda a, rows: signal_ref[a, rows, :].astype(jnp.float32), turns_ref, stacked, 0)

        def load_taps(a, rows):
            values = taps_ref[a, rows, :].astype(jnp.float32)
            return jnp.concatenate([values, jnp.zeros_like(values)], axis=1)

        stage_one(load_taps, turns_ref, stacked, LANES)

    sign = signs()
    all_spectra = [
        jnp.dot(table_ref[...], stacked[k * PER_STEP + sub], preferred_element_type=jnp.float32)
        for sub in range(PER_STEP)
    ]
    for sub, spectra in enumerate(all_spectra):
        signal_spec = spectra[:, :LANES]
        filter_low = spectra[:, LANES:].astype(jnp.bfloat16)
        spec_ref[sub] = signal_spec.astype(jnp.bfloat16)
        filt_ref[sub] = filter_low
        filter_wide = filter_low.astype(jnp.float32)
        swapped = swap(filter_wide)
        first_half = lower_half((ROWS, LANES))
        filter_real = jnp.where(first_half, filter_wide, swapped)
        filter_imag = jnp.where(first_half, swapped, filter_wide)
        product = signal_spec * filter_real + times_i(signal_spec, sign) * filter_imag
        operand = jnp.concatenate([product, times_i(product, -sign)], axis=0).astype(jnp.bfloat16)
        half[k * PER_STEP + sub] = jnp.dot(table_ref[...], operand, preferred_element_type=jnp.float32).astype(
            jnp.bfloat16
        )

    @pl.when(k == FIRST // PER_STEP - 1)
    def _():
        def store(a, rows, values):
            conv_ref[a, rows, :] = values.astype(jnp.bfloat16)

        last_stage(half, turns_ref, 0, store)


def grad_kernel(gated_ref, spec_ref, filt_ref, table_ref, turns_ref, grad_ref, taps_ref,
                stacked, half):
    k = pl.program_id(0)

    @pl.when(k == 0)
    def _():
        stage_one(lambda a, rows: gated_ref[a, rows, :].astype(jnp.float32), turns_ref, stacked, 0)

    sign = signs()
    all_spectra = [
        jnp.dot(table_ref[...], stacked[k * PER_STEP + sub], preferred_element_type=jnp.float32)
        for sub in range(PER_STEP)
    ]
    for sub, spectra in enumerate(all_spectra):
        turned = times_i(spectra, sign)
        first_half = lower_half((ROWS, LANES))

        def split(values):
            swapped = swap(values)
            return jnp.where(first_half, values, swapped), jnp.where(first_half, swapped, values)

        filter_real, filter_imag = split(filt_ref[sub].astype(jnp.float32))
        signal_real, signal_imag = split(spec_ref[sub].astype(jnp.float32))
        back = spectra * filter_real - turned * filter_imag
        cross = spectra * signal_real - turned * signal_imag
        operand = jnp.concatenate(
            [
                jnp.concatenate([back, cross], axis=1),
                jnp.concatenate([times_i(back, -sign), times_i(cross, -sign)], axis=1),
            ],
            axis=0,
        ).astype(jnp.bfloat16)
        half[k * PER_STEP + sub] = jnp.dot(table_ref[...], operand, preferred_element_type=jnp.float32).astype(
            jnp.bfloat16
        )

    @pl.when(k == FIRST // PER_STEP - 1)
    def _():
        def store(a, rows, values):
            grad_ref[a, rows, :] = values.astype(jnp.bfloat16)

        def store_taps(a, rows, values):
            taps_ref[a, rows, :] = values[:, :HALF].astype(jnp.bfloat16)

        last_stage(half, turns_ref, 0, store)
        last_stage(half, turns_ref, LANES, store_taps)


def whole_spec(shape):
    return pl.BlockSpec(shape, lambda k: (0,) * len(shape))


def each_spec(shape):
    return pl.BlockSpec((PER_STEP,) + shape, lambda k: (k,) + (0,) * len(shape))


TABLE_SPECS = [whole_spec((ROWS, 2 * ROWS)), whole_spec((2, ROWS, LANES))]
PARAMS = pltpu.CompilerParams(vmem_limit_bytes=56 * 1024 * 1024)
WORK = 2 * FIRST * ROWS * 2 * ROWS * 2 * LANES * 2
COST = pl.CostEstimate(flops=WORK, bytes_accessed=60 * 1024 * 1024, transcendentals=0)


def conv_call(signal_blocks, taps_blocks, table, turns):
    block = (CTX, ROWS, LANES)
    return pl.pallas_call(
        conv_kernel,
        grid=(FIRST // PER_STEP,),
        in_specs=[whole_spec(block), whole_spec((CTX, ROWS, HALF))] + TABLE_SPECS,
        out_specs=[whole_spec(block), each_spec((ROWS, LANES)), each_spec((ROWS, LANES))],
        out_shape=[
            jax.ShapeDtypeStruct(block, jnp.bfloat16),
            jax.ShapeDtypeStruct((FIRST, ROWS, LANES), jnp.bfloat16),
            jax.ShapeDtypeStruct((FIRST, ROWS, LANES), jnp.bfloat16),
        ],
        scratch_shapes=[
            pltpu.VMEM((FIRST, 2 * ROWS, 2 * LANES), jnp.bfloat16),
            pltpu.VMEM((FIRST, ROWS, LANES), jnp.bfloat16),
        ],
        compiler_params=PARAMS,
        cost_estimate=COST,
        name="conv_part",
    )(signal_blocks, taps_blocks, table, turns)


def grad_call(gated_blocks, spec, filt, table, turns):
    block = (CTX, ROWS, LANES)
    return pl.pallas_call(
        grad_kernel,
        grid=(FIRST // PER_STEP,),
        in_specs=[
            whole_spec(block),
            each_spec((ROWS, LANES)),
            each_spec((ROWS, LANES)),
        ]
        + TABLE_SPECS,
        out_specs=[whole_spec(block), whole_spec((CTX, ROWS, HALF))],
        out_shape=[
            jax.ShapeDtypeStruct(block, jnp.bfloat16),
            jax.ShapeDtypeStruct((CTX, ROWS, HALF), jnp.bfloat16),
        ],
        scratch_shapes=[
            pltpu.VMEM((FIRST, 2 * ROWS, LANES), jnp.bfloat16),
            pltpu.VMEM((FIRST, ROWS, 2 * LANES), jnp.bfloat16),
        ],
        compiler_params=PARAMS,
        cost_estimate=COST,
        name="grad_part",
    )(gated_blocks, spec, filt, table, turns)


def pack_pair(values, p):
    offset = CTX * HALF
    return jnp.concatenate(
        [values[:, HALF * p : HALF * p + HALF], values[:, offset + HALF * p : offset + HALF * p + HALF]],
        axis=1,
    )


def pack_kernel(signal_ref, packed_ref):
    values = signal_ref[...].astype(jnp.float32)
    for p in range(CTX):
        packed_ref[p] = pack_pair(values, p).astype(jnp.bfloat16)


def pack_gated_kernel(gate_ref, cotangent_ref, packed_ref):
    values = cotangent_ref[...].astype(jnp.float32) * gate_ref[...].astype(jnp.float32)
    for p in range(CTX):
        packed_ref[p] = pack_pair(values, p).astype(jnp.bfloat16)


PACK_ROWS = 128


def row_spec(width):
    return pl.BlockSpec((PACK_ROWS, width), lambda i: (i, 0))


def packed_spec():
    return pl.BlockSpec((CTX, PACK_ROWS, LANES), lambda i: (0, i, 0))


def pack_call(body, arrays):
    return pl.pallas_call(
        body,
        grid=(ROWS // PACK_ROWS,),
        in_specs=[row_spec(array.shape[1]) for array in arrays],
        out_specs=packed_spec(),
        out_shape=jax.ShapeDtypeStruct((CTX, ROWS, LANES), jnp.bfloat16),
        name="pack",
    )(*arrays)


def unpack(ref):
    blocks = [ref[p].astype(jnp.float32) for p in range(CTX)]
    return jnp.concatenate(
        [block[:, :HALF] for block in blocks] + [block[:, HALF:] for block in blocks], axis=1
    )


def outputs_kernel(conv_ref, signal_ref, gate_ref, cotangent_ref, gain_ref, output_ref, gate_out_ref):
    conv = unpack(conv_ref) + gain_ref[...] * signal_ref[...].astype(jnp.float32)
    output_ref[...] = (gate_ref[...].astype(jnp.float32) * conv).astype(jnp.bfloat16)
    gate_out_ref[...] = (cotangent_ref[...].astype(jnp.float32) * conv).astype(jnp.bfloat16)


def signal_grad_kernel(grad_ref, gate_ref, cotangent_ref, gain_ref, out_ref):
    gated = (cotangent_ref[...].astype(jnp.float32) * gate_ref[...].astype(jnp.float32)).astype(
        jnp.bfloat16
    )
    out_ref[...] = (unpack(grad_ref) + gain_ref[...] * gated.astype(jnp.float32)).astype(jnp.bfloat16)


def finish_call(body, packed, arrays, gain, count):
    width = gain.shape[1]
    return pl.pallas_call(
        body,
        grid=(ROWS // PACK_ROWS,),
        in_specs=[packed_spec()]
        + [row_spec(width)] * len(arrays)
        + [pl.BlockSpec((1, width), lambda i: (0, 0))],
        out_specs=[row_spec(width)] * count,
        out_shape=[jax.ShapeDtypeStruct((ROWS, width), jnp.bfloat16)] * count,
        name="finish",
    )(packed, *arrays, gain)


def exchange(blocks):
    return lax.all_to_all(blocks, "ctx", split_axis=0, concat_axis=0, tiled=True)


def gather_taps(taps):
    groups = lax.axis_size("grp")
    own = lax.axis_index("grp")
    width = taps.shape[1]
    pieces = [taps] + [
        lax.ppermute(taps, "grp", [(g, (g + step) % groups) for g in range(groups)])
        for step in range(1, groups)
    ]
    gathered = jnp.zeros((taps.shape[0], groups * width), taps.dtype)
    for step, piece in enumerate(pieces):
        start = lax.rem(own + (groups - step), groups) * width
        gathered = lax.dynamic_update_slice_in_dim(gathered, piece, start, axis=1)
    return gathered


def per_device(signal, gate, filter_taps, skip_gain, out_cotangent):
    filters = filter_taps.shape[1] * lax.axis_size("grp")
    if (
        lax.axis_size("ctx") != CTX
        or signal.shape != (ROWS, 2 * filters)
        or filters != CTX * HALF
    ):
        return per_device_general(signal, gate, filter_taps, skip_gain, out_cotangent)
    table, turns = (jnp.asarray(table) for table in dense_tables())
    gain = skip_gain[None, :]
    all_taps = gather_taps(filter_taps)
    taps_blocks = exchange(all_taps.reshape(ROWS, CTX, HALF).transpose(1, 0, 2))
    signal_blocks = exchange(pack_call(pack_kernel, [signal]))
    gated_blocks = exchange(pack_call(pack_gated_kernel, [gate, out_cotangent]))
    conv, spec, filt = conv_call(signal_blocks, taps_blocks, table, turns)
    conv_back = exchange(conv)
    grad, taps_grad = grad_call(gated_blocks, spec, filt, table, turns)
    grad, taps_grad, conv_back = lax.optimization_barrier((grad, taps_grad, conv_back))
    taps_back = exchange(taps_grad).transpose(1, 0, 2).reshape(ROWS, filters)
    grad_back = exchange(grad)
    output, grad_gate = finish_call(
        outputs_kernel, conv_back, [signal, gate, out_cotangent], gain, 2
    )
    (grad_signal,) = finish_call(signal_grad_kernel, grad_back, [gate, out_cotangent], gain, 1)
    scale = 1.0 / math.sqrt(CTX * ROWS * signal.shape[1] * lax.axis_size("grp") / filters)
    grad_filter = lax.psum_scatter(taps_back, "grp", scatter_dimension=1, tiled=True)
    return (output, grad_gate, grad_signal, grad_filter.astype(jnp.float32) * scale)


def solution(mesh):
    placed = (P("ctx", "grp"), P("ctx", "grp"), P("ctx", "grp"), P("grp"), P("ctx", "grp"))
    return jax.shard_map(
        per_device,
        mesh=mesh,
        in_specs=placed,
        out_specs=(P("ctx", "grp"), P("ctx", "grp"), P("ctx", "grp"), P("ctx", "grp")),
        check_vma=False,
    )
```

```python
import math

import jax
import jax.numpy as jnp
import ml_dtypes
import numpy as np
from jax import lax
from jax.experimental import pallas as pl
from jax.experimental.pallas import tpu as pltpu
from jax.sharding import PartitionSpec as P

TWO_PI = 2.0 * math.pi


def phase_pair(first_index, second_index, length):
    products_mod = first_index[:, None] * second_index[None, :] % length
    angles = products_mod.astype(jnp.float32) * (TWO_PI / length)
    return (jnp.cos(angles), -jnp.sin(angles))


def build_tables(devices_count, block_length, table_type):
    first_length = 2 * devices_count
    cosine_first, sine_first = phase_pair(
        jnp.arange(first_length, dtype=jnp.int32),
        jnp.arange(devices_count, dtype=jnp.int32),
        first_length,
    )
    stacked_rows = jnp.concatenate([cosine_first, sine_first], axis=0).astype(table_type)
    paired_rows = jnp.stack([cosine_first, sine_first], axis=0).astype(table_type)
    cosine_rows, sine_rows = phase_pair(
        jnp.arange(block_length, dtype=jnp.int32),
        jnp.arange(block_length, dtype=jnp.int32),
        block_length,
    )
    return (stacked_rows, paired_rows, cosine_rows.astype(table_type), sine_rows.astype(table_type))


def rotate_forward(first_out, first_freq, within_block, padded):
    half_rows = first_out.shape[0] // 2
    real_part = first_out[:half_rows]
    imag_part = first_out[half_rows:]
    twiddle_real, twiddle_imag = phase_pair(first_freq, within_block, padded)
    twiddle_real = twiddle_real[:, :, None]
    twiddle_imag = twiddle_imag[:, :, None]
    return jnp.stack(
        [
            real_part * twiddle_real - imag_part * twiddle_imag,
            real_part * twiddle_imag + imag_part * twiddle_real,
        ]
    )


def second_forward(rotated, cosine_rows, sine_rows):
    with_cosine = jnp.einsum(
        "jb,pkbc->pkjc", cosine_rows, rotated, preferred_element_type=jnp.float32
    )
    with_sine = jnp.einsum("jb,pkbc->pkjc", sine_rows, rotated, preferred_element_type=jnp.float32)
    return jnp.stack([with_cosine[0] - with_sine[1], with_cosine[1] + with_sine[0]])


def inverse_front(spectra, cosine_rows, sine_rows, first_freq, padded, precise):
    precision = lax.Precision.HIGHEST if precise else None
    operand = spectra if precise else spectra.astype(jnp.bfloat16)
    with_cosine = jnp.einsum(
        "jb,pkjc->pkbc",
        cosine_rows,
        operand,
        preferred_element_type=jnp.float32,
        precision=precision,
    )
    with_sine = jnp.einsum(
        "jb,pkjc->pkbc", sine_rows, operand, preferred_element_type=jnp.float32, precision=precision
    )
    real_turned = with_cosine[0] + with_sine[1]
    imag_turned = with_cosine[1] - with_sine[0]
    twiddle_real, twiddle_imag = phase_pair(
        first_freq, jnp.arange(spectra.shape[2], dtype=jnp.int32), padded
    )
    twiddle_real = twiddle_real[:, :, None]
    twiddle_imag = twiddle_imag[:, :, None]
    rotated = jnp.stack(
        [
            real_turned * twiddle_real + imag_turned * twiddle_imag,
            imag_turned * twiddle_real - real_turned * twiddle_imag,
        ]
    )
    if precise:
        return rotated
    return rotated.astype(jnp.bfloat16)


def inverse_back(rotated, paired_rows, padded, precise):
    precision = lax.Precision.HIGHEST if precise else None
    rows_out = jnp.einsum(
        "pka,pkbc->abc",
        paired_rows,
        rotated,
        preferred_element_type=jnp.float32,
        precision=precision,
    )
    return rows_out * (1.0 / padded)


def spectral_products(spectra, filter_low, width):
    filter_wide = filter_low.astype(jnp.float32)
    filter_real = filter_wide[0]
    filter_imag = filter_wide[1]
    input_real = spectra[0, ..., :width]
    input_imag = spectra[1, ..., :width]
    grad_real = spectra[0, ..., width:]
    grad_imag = spectra[1, ..., width:]
    channel_terms = jnp.stack(
        [
            jnp.concatenate(
                [
                    input_real * filter_real - input_imag * filter_imag,
                    grad_real * filter_real + grad_imag * filter_imag,
                ],
                axis=-1,
            ),
            jnp.concatenate(
                [
                    input_real * filter_imag + input_imag * filter_real,
                    grad_imag * filter_real - grad_real * filter_imag,
                ],
                axis=-1,
            ),
        ]
    )
    filter_term = jnp.stack(
        [
            input_real * grad_real + input_imag * grad_imag,
            input_real * grad_imag - input_imag * grad_real,
        ]
    )
    return (channel_terms, filter_term)


def split_forward(values, tables, position):
    stacked_rows, paired_rows, cosine_rows, sine_rows = tables
    devices_count = lax.axis_size("ctx")
    block_length = values.shape[0]
    lane_count = block_length // devices_count
    padded = 2 * devices_count * block_length
    first_length = 2 * devices_count
    first_out = jnp.einsum(
        "ka,abc->kbc",
        stacked_rows,
        lax.all_to_all(values[None], "ctx", split_axis=1, concat_axis=0, tiled=True),
        preferred_element_type=jnp.float32,
    )
    within_block = position * lane_count + jnp.arange(lane_count, dtype=jnp.int32)
    rotated = rotate_forward(
        first_out, jnp.arange(first_length, dtype=jnp.int32), within_block, padded
    ).astype(jnp.bfloat16)
    return second_forward(
        lax.all_to_all(rotated, "ctx", split_axis=1, concat_axis=2, tiled=True),
        cosine_rows,
        sine_rows,
    )


def split_inverse(spectra, tables, position, precise):
    stacked_rows, paired_rows, cosine_rows, sine_rows = tables
    devices_count = lax.axis_size("ctx")
    freq_count = spectra.shape[1]
    padded = 2 * devices_count * spectra.shape[2]
    first_freq = position * freq_count + jnp.arange(freq_count, dtype=jnp.int32)
    rotated = inverse_front(spectra, cosine_rows, sine_rows, first_freq, padded, precise)
    if precise:
        last_rows_out = inverse_back(
            lax.all_to_all(
                rotated.astype(jnp.bfloat16), "ctx", split_axis=2, concat_axis=1, tiled=True
            ).astype(rotated.dtype),
            paired_rows,
            padded,
            True,
        )
        result = lax.all_to_all(
            last_rows_out.astype(jnp.bfloat16), "ctx", split_axis=0, concat_axis=1, tiled=True
        ).astype(last_rows_out.dtype)
    else:
        rows_out = inverse_back(
            lax.all_to_all(rotated, "ctx", split_axis=2, concat_axis=1, tiled=True),
            paired_rows,
            padded,
            False,
        )
        result = lax.all_to_all(
            rows_out.astype(jnp.bfloat16), "ctx", split_axis=0, concat_axis=1, tiled=True
        ).astype(rows_out.dtype)
    return result[0]


def per_device_general(signal, gate, filter_taps, skip_gain, out_cotangent):
    devices_count = lax.axis_size("ctx")
    group_count = lax.axis_size("grp")
    block_length = signal.shape[0]
    local_channels = signal.shape[1]
    filters = filter_taps.shape[1] * group_count
    repeats = local_channels // filters
    position = lax.axis_index("ctx")
    coarse_tables = build_tables(devices_count, block_length, jnp.bfloat16)
    exact_tables = build_tables(devices_count, block_length, jnp.float32)
    gated = (out_cotangent.astype(jnp.float32) * gate.astype(jnp.float32)).astype(jnp.bfloat16)
    gain_wide = skip_gain[None, :]
    all_filters = lax.all_gather(filter_taps, "grp", axis=1, tiled=True)
    filter_low = lax.optimization_barrier(
        split_forward(all_filters, coarse_tables, position).astype(jnp.bfloat16)
    )
    filter_totals = jnp.zeros((2, 2, block_length, filters), jnp.float32)
    conv_blocks = []
    grad_blocks = []
    for block_index in range(repeats):
        lower = block_index * filters
        columns = jnp.concatenate(
            [signal[:, lower : lower + filters], gated[:, lower : lower + filters]], axis=1
        )
        spectra = split_forward(columns, coarse_tables, position)
        channel_terms, filter_term = spectral_products(spectra, filter_low, filters)
        filter_totals = filter_totals + filter_term
        signal_back = split_inverse(channel_terms, coarse_tables, position, False)
        conv_blocks.append(signal_back[:, :filters])
        grad_blocks.append(signal_back[:, filters:])
    conv_part = jnp.concatenate(conv_blocks, axis=1)
    grad_conv = jnp.concatenate(grad_blocks, axis=1)
    filter_back = split_inverse(filter_totals, exact_tables, position, True)
    grad_filter = lax.psum_scatter(
        filter_back.astype(jnp.bfloat16), "grp", scatter_dimension=1, tiled=True
    ).astype(jnp.float32)
    conv_part = conv_part + gain_wide * signal.astype(jnp.float32)
    output = (gate.astype(jnp.float32) * conv_part).astype(jnp.bfloat16)
    grad_gate = (out_cotangent.astype(jnp.float32) * conv_part).astype(jnp.bfloat16)
    grad_signal = (grad_conv + gain_wide * gated.astype(jnp.float32)).astype(jnp.bfloat16)
    scale = 1.0 / math.sqrt(devices_count * block_length * local_channels * group_count / filters)
    return (output, grad_gate, grad_signal, grad_filter * scale)


CTX = 8
FIRST = 16
ROWS = 512
LANES = 128
HALF = 64
STRIP = 16
PER_STEP = 4


def low(values):
    return np.asarray(values, np.float32).astype(ml_dtypes.bfloat16)


def first_coefficients():
    index = np.arange(FIRST)
    angles = (index[:, None] * index[None, :] % FIRST).astype(np.float32) * np.float32(TWO_PI / FIRST)
    return (
        low(np.round(np.cos(angles), 7)).astype(np.float64),
        low(np.round(np.sin(angles), 7)).astype(np.float64),
    )


def dense_tables():
    index = np.arange(ROWS)
    angles = (index[:, None] * index[None, :] % ROWS).astype(np.float32) * np.float32(TWO_PI / ROWS)
    table = low(np.concatenate([np.cos(angles), -np.sin(angles)], axis=1))
    turn = index * (TWO_PI / (FIRST * ROWS))
    turns = np.stack([np.cos(turn), -np.sin(turn)])[:, :, None]
    return table, np.broadcast_to(turns, (2, ROWS, LANES)).astype(np.float32)


COS, SIN = first_coefficients()


def scaled_sum(terms):
    total = None
    for coefficient, value in terms:
        coefficient = float(coefficient)
        if abs(coefficient) < 1e-6:
            continue
        if total is None:
            total = value if coefficient == 1.0 else value * coefficient
        elif coefficient == 1.0:
            total = total + value
        elif coefficient == -1.0:
            total = total - value
        else:
            total = total + value * coefficient
    return total


def lower_half(shape):
    return lax.broadcasted_iota(jnp.int32, shape, len(shape) - 1) < HALF


def swap(values):
    return pltpu.roll(values, HALF, axis=1)


def times_i(values, sign):
    return swap(values) * sign


def forward_first(blocks, sign):
    plus = {a: blocks[a] + blocks[8 - a] for a in (1, 2, 3)}
    minus = {a: blocks[a] - blocks[8 - a] for a in (1, 2, 3)}
    results = [None] * FIRST
    for k in range(9):
        if k % 2 == 0:
            real = scaled_sum(
                [(1.0, blocks[0]), (COS[k, 4], blocks[4])] + [(COS[k, a], plus[a]) for a in (1, 2, 3)]
            )
            turned = scaled_sum([(-SIN[k, a], minus[a]) for a in (1, 2, 3)])
        else:
            real = scaled_sum([(1.0, blocks[0])] + [(COS[k, a], minus[a]) for a in (1, 2, 3)])
            turned = scaled_sum([(-SIN[k, 4], blocks[4])] + [(-SIN[k, a], plus[a]) for a in (1, 2, 3)])
        real_turned = times_i(real, sign)
        if turned is None:
            results[k] = (real, real_turned)
            continue
        twice = times_i(turned, sign)
        results[k] = (real + twice, real_turned - turned)
        results[FIRST - k] = (real - twice, real_turned + turned)
    return results


def inverse_last(parts, sign):
    even = {k: parts[k] + parts[FIRST - k] for k in range(1, 8)}
    odd = {k: parts[k] - parts[FIRST - k] for k in range(1, 8)}
    results = [None] * CTX
    for a in range(5):
        flip = 1.0 if a % 2 == 0 else -1.0
        real_even = scaled_sum(
            [(1.0, parts[0]), (flip, parts[8])] + [(COS[k, a], even[k]) for k in (2, 4, 6)]
        )
        real_odd = scaled_sum([(COS[k, a], even[k]) for k in (1, 3, 5, 7)])
        turn_even = scaled_sum([(SIN[k, a], odd[k]) for k in (2, 4, 6)])
        turn_odd = scaled_sum([(SIN[k, a], odd[k]) for k in (1, 3, 5, 7)])
        real = real_even if real_odd is None else real_even + real_odd
        if a == 0:
            results[0] = real
            continue
        if a == 4:
            results[4] = real + times_i(turn_odd, sign)
            continue
        results[a] = real + times_i(turn_even + turn_odd, sign)
        results[8 - a] = (real_even - real_odd) + times_i(turn_odd - turn_even, sign)
    return results


def signs():
    return jnp.where(lower_half((1, LANES)), -1.0, 1.0).astype(jnp.float32)


def next_turn(turn, unit):
    return (turn[0] * unit[0] - turn[1] * unit[1], turn[0] * unit[1] + turn[1] * unit[0])


def stage_one(load, turns_ref, stacked_ref, lane_start):
    sign = signs()

    @pl.loop(0, ROWS // STRIP)
    def _(strip):
        rows = pl.multiple_of(strip * STRIP, STRIP)
        blocks = [load(a, pl.ds(rows, STRIP)) for a in range(CTX)]
        unit = (turns_ref[0, pl.ds(rows, STRIP), :], turns_ref[1, pl.ds(rows, STRIP), :])
        lanes = slice(lane_start, lane_start + LANES)
        turn = None
        for k, (values, turned) in enumerate(forward_first(blocks, sign)):
            if k > 0:
                turn = unit if turn is None else next_turn(turn, unit)
                values, turned = (
                    values * turn[0] + turned * turn[1],
                    turned * turn[0] - values * turn[1],
                )
            stacked_ref[k, pl.ds(rows, STRIP), lanes] = values.astype(jnp.bfloat16)
            stacked_ref[k, pl.ds(ROWS + rows, STRIP), lanes] = turned.astype(jnp.bfloat16)


def last_stage(half_ref, turns_ref, lane_start, store):
    sign = signs()

    @pl.loop(0, ROWS // STRIP)
    def _(strip):
        rows = pl.multiple_of(strip * STRIP, STRIP)
        unit = (turns_ref[0, pl.ds(rows, STRIP), :], turns_ref[1, pl.ds(rows, STRIP), :])
        turn = (1.0 / (FIRST * ROWS), 0.0)
        parts = []
        for k in range(FIRST):
            part = half_ref[k, pl.ds(rows, STRIP), lane_start : lane_start + LANES].astype(
                jnp.float32
            )
            if k == 0:
                parts.append(part * turn[0])
                continue
            turn = (turn[0] * unit[0], turn[0] * unit[1]) if k == 1 else next_turn(turn, unit)
            parts.append(part * turn[0] - times_i(part, sign) * turn[1])
        for a, values in enumerate(inverse_last(parts, sign)):
            store(a, pl.ds(rows, STRIP), values)


def conv_kernel(signal_ref, taps_ref, table_ref, turns_ref, conv_ref, spec_ref, filt_ref,
                stacked, half):
    k = pl.program_id(0)

    @pl.when(k == 0)
    def _():
        stage_one(lambda a, rows: signal_ref[a, rows, :].astype(jnp.float32), turns_ref, stacked, 0)

        def load_taps(a, rows):
            values = taps_ref[a, rows, :].astype(jnp.float32)
            return jnp.concatenate([values, jnp.zeros_like(values)], axis=1)

        stage_one(load_taps, turns_ref, stacked, LANES)

    sign = signs()
    all_spectra = [
        jnp.dot(table_ref[...], stacked[k * PER_STEP + sub], preferred_element_type=jnp.float32)
        for sub in range(PER_STEP)
    ]
    for sub, spectra in enumerate(all_spectra):
        signal_spec = spectra[:, :LANES]
        filter_low = spectra[:, LANES:].astype(jnp.bfloat16)
        spec_ref[sub] = signal_spec.astype(jnp.bfloat16)
        filt_ref[sub] = filter_low
        filter_wide = filter_low.astype(jnp.float32)
        swapped = swap(filter_wide)
        first_half = lower_half((ROWS, LANES))
        filter_real = jnp.where(first_half, filter_wide, swapped)
        filter_imag = jnp.where(first_half, swapped, filter_wide)
        product = signal_spec * filter_real + times_i(signal_spec, sign) * filter_imag
        operand = jnp.concatenate([product, times_i(product, -sign)], axis=0).astype(jnp.bfloat16)
        half[k * PER_STEP + sub] = jnp.dot(table_ref[...], operand, preferred_element_type=jnp.float32).astype(
            jnp.bfloat16
        )

    @pl.when(k == FIRST // PER_STEP - 1)
    def _():
        def store(a, rows, values):
            conv_ref[a, rows, :] = values.astype(jnp.bfloat16)

        last_stage(half, turns_ref, 0, store)


def grad_kernel(gated_ref, spec_ref, filt_ref, table_ref, turns_ref, grad_ref, taps_ref,
                stacked, half):
    k = pl.program_id(0)

    @pl.when(k == 0)
    def _():
        stage_one(lambda a, rows: gated_ref[a, rows, :].astype(jnp.float32), turns_ref, stacked, 0)

    sign = signs()
    all_spectra = [
        jnp.dot(table_ref[...], stacked[k * PER_STEP + sub], preferred_element_type=jnp.float32)
        for sub in range(PER_STEP)
    ]
    for sub, spectra in enumerate(all_spectra):
        turned = times_i(spectra, sign)
        first_half = lower_half((ROWS, LANES))

        def split(values):
            swapped = swap(values)
            return jnp.where(first_half, values, swapped), jnp.where(first_half, swapped, values)

        filter_real, filter_imag = split(filt_ref[sub].astype(jnp.float32))
        signal_real, signal_imag = split(spec_ref[sub].astype(jnp.float32))
        back = spectra * filter_real - turned * filter_imag
        cross = spectra * signal_real - turned * signal_imag
        operand = jnp.concatenate(
            [
                jnp.concatenate([back, cross], axis=1),
                jnp.concatenate([times_i(back, -sign), times_i(cross, -sign)], axis=1),
            ],
            axis=0,
        ).astype(jnp.bfloat16)
        half[k * PER_STEP + sub] = jnp.dot(table_ref[...], operand, preferred_element_type=jnp.float32).astype(
            jnp.bfloat16
        )

    @pl.when(k == FIRST // PER_STEP - 1)
    def _():
        def store(a, rows, values):
            grad_ref[a, rows, :] = values.astype(jnp.bfloat16)

        def store_taps(a, rows, values):
            taps_ref[a, rows, :] = values[:, :HALF].astype(jnp.bfloat16)

        last_stage(half, turns_ref, 0, store)
        last_stage(half, turns_ref, LANES, store_taps)


def whole_spec(shape):
    return pl.BlockSpec(shape, lambda k: (0,) * len(shape))


def each_spec(shape):
    return pl.BlockSpec((PER_STEP,) + shape, lambda k: (k,) + (0,) * len(shape))


TABLE_SPECS = [whole_spec((ROWS, 2 * ROWS)), whole_spec((2, ROWS, LANES))]
PARAMS = pltpu.CompilerParams(vmem_limit_bytes=56 * 1024 * 1024)
WORK = 2 * FIRST * ROWS * 2 * ROWS * 2 * LANES * 2
COST = pl.CostEstimate(flops=WORK, bytes_accessed=60 * 1024 * 1024, transcendentals=0)


def conv_call(signal_blocks, taps_blocks, table, turns):
    block = (CTX, ROWS, LANES)
    return pl.pallas_call(
        conv_kernel,
        grid=(FIRST // PER_STEP,),
        in_specs=[whole_spec(block), whole_spec((CTX, ROWS, HALF))] + TABLE_SPECS,
        out_specs=[whole_spec(block), each_spec((ROWS, LANES)), each_spec((ROWS, LANES))],
        out_shape=[
            jax.ShapeDtypeStruct(block, jnp.bfloat16),
            jax.ShapeDtypeStruct((FIRST, ROWS, LANES), jnp.bfloat16),
            jax.ShapeDtypeStruct((FIRST, ROWS, LANES), jnp.bfloat16),
        ],
        scratch_shapes=[
            pltpu.VMEM((FIRST, 2 * ROWS, 2 * LANES), jnp.bfloat16),
            pltpu.VMEM((FIRST, ROWS, LANES), jnp.bfloat16),
        ],
        compiler_params=PARAMS,
        cost_estimate=COST,
        name="conv_part",
    )(signal_blocks, taps_blocks, table, turns)


def grad_call(gated_blocks, spec, filt, table, turns):
    block = (CTX, ROWS, LANES)
    return pl.pallas_call(
        grad_kernel,
        grid=(FIRST // PER_STEP,),
        in_specs=[
            whole_spec(block),
            each_spec((ROWS, LANES)),
            each_spec((ROWS, LANES)),
        ]
        + TABLE_SPECS,
        out_specs=[whole_spec(block), whole_spec((CTX, ROWS, HALF))],
        out_shape=[
            jax.ShapeDtypeStruct(block, jnp.bfloat16),
            jax.ShapeDtypeStruct((CTX, ROWS, HALF), jnp.bfloat16),
        ],
        scratch_shapes=[
            pltpu.VMEM((FIRST, 2 * ROWS, LANES), jnp.bfloat16),
            pltpu.VMEM((FIRST, ROWS, 2 * LANES), jnp.bfloat16),
        ],
        compiler_params=PARAMS,
        cost_estimate=COST,
        name="grad_part",
    )(gated_blocks, spec, filt, table, turns)


def pack_pair(values, p):
    offset = CTX * HALF
    return jnp.concatenate(
        [values[:, HALF * p : HALF * p + HALF], values[:, offset + HALF * p : offset + HALF * p + HALF]],
        axis=1,
    )


def pack_kernel(signal_ref, packed_ref):
    values = signal_ref[...].astype(jnp.float32)
    for p in range(CTX):
        packed_ref[p] = pack_pair(values, p).astype(jnp.bfloat16)


def pack_gated_kernel(gate_ref, cotangent_ref, packed_ref):
    values = cotangent_ref[...].astype(jnp.float32) * gate_ref[...].astype(jnp.float32)
    for p in range(CTX):
        packed_ref[p] = pack_pair(values, p).astype(jnp.bfloat16)


PACK_ROWS = 128


def row_spec(width):
    return pl.BlockSpec((PACK_ROWS, width), lambda i: (i, 0))


def packed_spec():
    return pl.BlockSpec((CTX, PACK_ROWS, LANES), lambda i: (0, i, 0))


def pack_call(body, arrays):
    return pl.pallas_call(
        body,
        grid=(ROWS // PACK_ROWS,),
        in_specs=[row_spec(array.shape[1]) for array in arrays],
        out_specs=packed_spec(),
        out_shape=jax.ShapeDtypeStruct((CTX, ROWS, LANES), jnp.bfloat16),
        name="pack",
    )(*arrays)


def unpack(ref):
    blocks = [ref[p].astype(jnp.float32) for p in range(CTX)]
    return jnp.concatenate(
        [block[:, :HALF] for block in blocks] + [block[:, HALF:] for block in blocks], axis=1
    )


def outputs_kernel(conv_ref, signal_ref, gate_ref, cotangent_ref, gain_ref, output_ref, gate_out_ref):
    conv = unpack(conv_ref) + gain_ref[...] * signal_ref[...].astype(jnp.float32)
    output_ref[...] = (gate_ref[...].astype(jnp.float32) * conv).astype(jnp.bfloat16)
    gate_out_ref[...] = (cotangent_ref[...].astype(jnp.float32) * conv).astype(jnp.bfloat16)


def signal_grad_kernel(grad_ref, gate_ref, cotangent_ref, gain_ref, out_ref):
    gated = (cotangent_ref[...].astype(jnp.float32) * gate_ref[...].astype(jnp.float32)).astype(
        jnp.bfloat16
    )
    out_ref[...] = (unpack(grad_ref) + gain_ref[...] * gated.astype(jnp.float32)).astype(jnp.bfloat16)


def finish_call(body, packed, arrays, gain, count):
    width = gain.shape[1]
    return pl.pallas_call(
        body,
        grid=(ROWS // PACK_ROWS,),
        in_specs=[packed_spec()]
        + [row_spec(width)] * len(arrays)
        + [pl.BlockSpec((1, width), lambda i: (0, 0))],
        out_specs=[row_spec(width)] * count,
        out_shape=[jax.ShapeDtypeStruct((ROWS, width), jnp.bfloat16)] * count,
        name="finish",
    )(packed, *arrays, gain)


def exchange(blocks):
    return lax.all_to_all(blocks, "ctx", split_axis=0, concat_axis=0, tiled=True)


def gather_taps(taps, after):
    groups = lax.axis_size("grp")
    own = lax.axis_index("grp")
    width = taps.shape[1]
    pieces = [taps] + [
        lax.ppermute(taps, "grp", [(g, (g + step) % groups) for g in range(groups)])
        for step in range(1, groups)
    ]
    pieces, after = lax.optimization_barrier((pieces, after))
    gathered = jnp.zeros((taps.shape[0], groups * width), taps.dtype)
    for step, piece in enumerate(pieces):
        start = lax.rem(own + (groups - step), groups) * width
        gathered = lax.dynamic_update_slice_in_dim(gathered, piece, start, axis=1)
    return gathered, after


def per_device(signal, gate, filter_taps, skip_gain, out_cotangent):
    filters = filter_taps.shape[1] * lax.axis_size("grp")
    if (
        lax.axis_size("ctx") != CTX
        or signal.shape != (ROWS, 2 * filters)
        or filters != CTX * HALF
    ):
        return per_device_general(signal, gate, filter_taps, skip_gain, out_cotangent)
    table, turns = (jnp.asarray(table) for table in dense_tables())
    gain = skip_gain[None, :]
    signal_blocks = exchange(pack_call(pack_kernel, [signal]))
    all_taps, signal_blocks = gather_taps(filter_taps, signal_blocks)
    taps_blocks = exchange(all_taps.reshape(ROWS, CTX, HALF).transpose(1, 0, 2))
    gated_blocks = exchange(pack_call(pack_gated_kernel, [gate, out_cotangent]))
    conv, spec, filt = conv_call(signal_blocks, taps_blocks, table, turns)
    conv_back = exchange(conv)
    grad, taps_grad = grad_call(gated_blocks, spec, filt, table, turns)
    grad, taps_grad, conv_back = lax.optimization_barrier((grad, taps_grad, conv_back))
    taps_back = exchange(taps_grad).transpose(1, 0, 2).reshape(ROWS, filters)
    grad_back = exchange(grad)
    output, grad_gate = finish_call(
        outputs_kernel, conv_back, [signal, gate, out_cotangent], gain, 2
    )
    (grad_signal,) = finish_call(signal_grad_kernel, grad_back, [gate, out_cotangent], gain, 1)
    scale = 1.0 / math.sqrt(CTX * ROWS * signal.shape[1] * lax.axis_size("grp") / filters)
    grad_filter = lax.psum_scatter(taps_back, "grp", scatter_dimension=1, tiled=True)
    return (output, grad_gate, grad_signal, grad_filter.astype(jnp.float32) * scale)


def solution(mesh):
    placed = (P("ctx", "grp"), P("ctx", "grp"), P("ctx", "grp"), P("grp"), P("ctx", "grp"))
    return jax.shard_map(
        per_device,
        mesh=mesh,
        in_specs=placed,
        out_specs=(P("ctx", "grp"), P("ctx", "grp"), P("ctx", "grp"), P("ctx", "grp")),
        check_vma=False,
    )
```
